512 devices in a mesh: wide: 64 (over z, y_hi, core), narrow: 8 (over y_lo, x).
Axes of the slice: x: 4, y: 8 (y_hi: 4, y_lo: 2; y = y_hi * 2 + y_lo), z: 8, core: 2. Of those that a mesh axis runs over, the one named last changes fastest.
Arguments:
- fields: float32 [5, 192, 64, 1024], P(None, 'wide', 'narrow'), may hold values from -6 to 6
- y_bands: float32 [3, 192], replicated, may hold values from -1.5 to 4, as said below
Outputs:
- new_fields: float32 [5, 192, 64, 1024], P(None, 'wide', 'narrow')
- pressure: float32 [192, 64, 1024], P('wide', 'narrow')
The draws below stay inside these ranges and needn't reach their ends.
Inputs may be any that keep to these rules, and one draw needn't show every extreme that they name: `y_bands`: row 0 holds the couplings to the row below (its first entry zero), row 1 the diagonal, row 2 the couplings to the row above (its last entry zero); the matrix is symmetric and each diagonal entry exceeds the sum of the magnitudes beside it.
All inputs are finite; a program needn't handle non-finite values.
Results may differ from the reference program's by a relative error of at most 0.0003.
Values sent between devices are 32-bit elements; how exact they have to be, the bound alone decides.
A program may use at most 128 MiB of HBM per device.

```python
import math
import jax
import jax.numpy as jnp
from jax import lax

NX = 1024
NZ = 64
CY = 3
NY = 192


def draw_y_bands(key, part):
    split_one, split_two = jax.random.split(key)
    coupling = jax.random.uniform(split_one, (NY + 1,), jnp.float32, 0.3, 1.5)
    shift = jnp.exp(jax.random.uniform(split_two, (NY,), jnp.float32, math.log(0.05), math.log(1.0)))
    nothing = jnp.zeros((1,), jnp.float32)
    lower = jnp.concatenate([nothing, -coupling[1:NY]])
    upper = jnp.concatenate([-coupling[1:NY], nothing])
    diagonal = coupling[:NY] + coupling[1:] + shift
    return jnp.stack([lower, diagonal, upper], 0)


def levels(own_key, shape, cuts, least, top_value):
    def one(axis_at, blocks):
        steps = jax.random.uniform(jax.random.fold_in(jax.random.fold_in(own_key, 6), axis_at), (blocks,), jnp.float32, least / len(cuts), top_value / len(cuts))
        return jnp.repeat(jnp.exp(steps), shape[axis_at] // blocks).reshape((-1,) + (1,) * (len(shape) - axis_at - 1))

    factor_of = one(*cuts[0])
    for cut in cuts[1:]:
        factor_of = factor_of * one(*cut)
    return factor_of


def gaussian(stream_key, dims, deviation, bound, pieces=(), held_as=jnp.bfloat16):
    entries = deviation * jax.random.normal(stream_key, dims, jnp.float32)
    if pieces:
        entries = entries * levels(stream_key, dims, pieces, -0.22, 0.18)
    return jnp.clip(entries, -bound, bound).astype(held_as)


def setup_inputs(seed: int = 0) -> dict:
    key_list = jax.random.split(jax.random.key(seed), 3)
    return {
        "fields": gaussian(key_list[0], (5, NY, NZ, NX), 1.0, 6.0, ((1, 64), (2, 8)), jnp.float32),
        "y_bands": draw_y_bands(jax.random.fold_in(key_list[2], 71), 0),
    }


EPSILON = 1e-06
STEP = 0.05
GRAVITY = 0.5
MOLECULAR = [0.02, 0.02, 0.02, 0.028, 0.04]
TURBULENT = [1.0, 1.0, 1.0, 1.0 / 0.85, 1.0 / 0.7]
PAIR_FIRST = [0, 1, 2, 0, 0, 1]
PAIR_SECOND = [0, 1, 2, 1, 2, 2]
PAIR_WEIGHTS = [1.0, 1.0, 1.0, 2.0, 2.0, 2.0]

def shrink(values, margin_w):
    return values[..., margin_w:values.shape[-3] - margin_w, margin_w:values.shape[-2] - margin_w, :]

def diff_x(values):
    middle = shrink(values, 1)
    return (jnp.roll(middle, -1, -1) - jnp.roll(middle, 1, -1)) * 0.5

def diff_y(values):
    return (values[..., 2:, 1:-1, :] - values[..., :-2, 1:-1, :]) * 0.5

def diff_z(values):
    return (values[..., 1:-1, 2:, :] - values[..., 1:-1, :-2, :]) * 0.5

def central(values):
    return (diff_x(values), diff_y(values), diff_z(values))

def fourth(values):
    middle = shrink(values, 2)
    along_x = (8.0 * (jnp.roll(middle, -1, -1) - jnp.roll(middle, 1, -1)) - (jnp.roll(middle, -2, -1) - jnp.roll(middle, 2, -1))) / 12.0
    along_y = (8.0 * (values[..., 3:-1, 2:-2, :] - values[..., 1:-3, 2:-2, :]) - (values[..., 4:, 2:-2, :] - values[..., :-4, 2:-2, :])) / 12.0
    along_z = (8.0 * (values[..., 2:-2, 3:-1, :] - values[..., 2:-2, 1:-3, :]) - (values[..., 2:-2, 4:, :] - values[..., 2:-2, :-4, :])) / 12.0
    return (along_x, along_y, along_z)

def laplace(values):
    middle = shrink(values, 1)
    total = jnp.roll(middle, -1, -1) + jnp.roll(middle, 1, -1)
    total = total + values[..., 2:, 1:-1, :] + values[..., :-2, 1:-1, :]
    total = total + values[..., 1:-1, 2:, :] + values[..., 1:-1, :-2, :]
    return total - 6.0 * middle

def smooth(values):
    passed = 0.25 * jnp.roll(values, -1, -1) + 0.5 * values + 0.25 * jnp.roll(values, 1, -1)
    passed = 0.25 * passed[..., :-2, :, :] + 0.5 * passed[..., 1:-1, :, :] + 0.25 * passed[..., 2:, :, :]
    return 0.25 * passed[..., :, :-2, :] + 0.5 * passed[..., :, 1:-1, :] + 0.25 * passed[..., :, 2:, :]

def pair_weights(dtype):
    return jnp.asarray(PAIR_WEIGHTS, dtype)[:, None, None, None]

def strain_of(velocity):
    grads = [central(velocity[index]) for index in range(3)]
    strain = jnp.stack([0.5 * (grads[first][second] + grads[second][first]) for first, second in zip(PAIR_FIRST, PAIR_SECOND)], 0)
    magnitude = jnp.sqrt(2.0 * lax.optimization_barrier(jnp.sum(pair_weights(strain.dtype) * strain * strain, 0)))
    return (strain, magnitude)

def closure(padded):
    velocity = padded[0:3]
    strain, magnitude = strain_of(velocity)
    filtered = smooth(velocity)
    products = smooth(jnp.stack([velocity[first] * velocity[second] for first, second in zip(PAIR_FIRST, PAIR_SECOND)], 0))
    filtered_products = jnp.stack([filtered[first] * filtered[second] for first, second in zip(PAIR_FIRST, PAIR_SECOND)], 0)
    leonard = shrink(products - filtered_products, 1)
    strain_hat, magnitude_hat = strain_of(filtered)
    modeled = 2.0 * (smooth(magnitude * strain) - 4.0 * magnitude_hat * strain_hat)
    weights = pair_weights(modeled.dtype)
    return (shrink(magnitude, 1), lax.optimization_barrier(jnp.sum(weights * leonard * modeled, 0)), lax.optimization_barrier(jnp.sum(weights * modeled * modeled, 0)))

def advance(padded, magnitude, coefficient):
    centre = shrink(padded, 2)
    along_x, along_y, along_z = fourth(padded)
    carried = centre[0] * along_x + centre[1] * along_y + centre[2] * along_z
    eddy_visc = coefficient[:, None, None] * magnitude
    molecular = jnp.asarray(MOLECULAR, padded.dtype)[:, None, None, None]
    turbulent = jnp.asarray(TURBULENT, padded.dtype)[:, None, None, None]
    tendency = -carried + (molecular + turbulent * eddy_visc) * laplace(shrink(padded, 1))
    buoyancy = jnp.concatenate([jnp.zeros_like(centre[0:1]), GRAVITY * centre[3:4], jnp.zeros_like(centre[0:3])], 0)
    return centre + STEP * (tendency + buoyancy)

def eigen(modes, count):
    half = count // 2
    wave = jnp.where(modes <= half, modes, modes - half).astype(jnp.float32)
    return 2.0 - 2.0 * jnp.cos(2.0 * math.pi / count * wave)

def forward_real(values, axis):
    count = values.shape[axis]
    half = count // 2
    spectrum = jnp.fft.rfft(values, axis=axis)
    cosines = spectrum.real
    sines = -lax.slice_in_dim(spectrum.imag, 1, half, axis=axis)
    return jnp.concatenate([cosines, sines], axis)

def inverse_real(coefs, axis):
    count = coefs.shape[axis]
    half = count // 2
    cosines = lax.slice_in_dim(coefs, 0, half + 1, axis=axis)
    sines = lax.slice_in_dim(coefs, half + 1, count, axis=axis)
    nothing = jnp.zeros_like(lax.slice_in_dim(coefs, 0, 1, axis=axis))
    sines = jnp.concatenate([nothing, sines, nothing], axis)
    return jnp.fft.irfft(cosines - 1j * sines, n=count, axis=axis)

def reference(fields, y_bands):
    padded = jnp.pad(fields, ((0, 0), (2, 2), (0, 0), (0, 0)))
    padded = jnp.pad(padded, ((0, 0), (0, 0), (2, 2), (0, 0)), mode='wrap')
    blocks = NY // CY
    indices = jnp.arange(blocks, dtype=jnp.int32)

    def window(index):
        return lax.dynamic_slice_in_dim(padded, (index * CY).astype(jnp.int32), CY + 4, 1)

    def plane_terms(index):
        magnitude, cross, square = closure(window(index))
        return (lax.optimization_barrier(jnp.sum(cross, (1, 2))), lax.optimization_barrier(jnp.sum(square, (1, 2))))
    cross_rows, square_rows = lax.map(plane_terms, indices)
    coefficient = (cross_rows / (square_rows + EPSILON)).reshape(-1)

    def step_block(index):
        window_rows = window(index)
        magnitude = closure(window_rows)[0]
        local = lax.dynamic_slice_in_dim(coefficient, (index * CY).astype(jnp.int32), CY)
        return advance(window_rows, magnitude, local)
    predicted = lax.map(step_block, indices)
    predicted = jnp.moveaxis(predicted, 0, 1).reshape(5, NY, NZ, NX)
    velocity = predicted[0:3]
    walled = jnp.pad(velocity, ((0, 0), (1, 1), (0, 0), (0, 0)))
    walled = jnp.pad(walled, ((0, 0), (0, 0), (1, 1), (0, 0)), mode='wrap')
    divergence = diff_x(walled[0]) + diff_y(walled[1]) + diff_z(walled[2])
    spectral = forward_real(forward_real(divergence, 2), 1)
    spectral = jnp.transpose(spectral, (2, 1, 0))
    eig = eigen(jnp.arange(NX, dtype=jnp.int32), NX)[:, None, None] + eigen(jnp.arange(NZ, dtype=jnp.int32), NZ)[None, :, None]
    diagonal = y_bands[1][None, None, :] + eig
    lower_band = jnp.broadcast_to(y_bands[0][None, None, :], diagonal.shape)
    upper_band = jnp.broadcast_to(y_bands[2][None, None, :], diagonal.shape)
    solved = lax.linalg.tridiagonal_solve(lower_band, diagonal, upper_band, -spectral[..., None])[..., 0]
    pressure = inverse_real(inverse_real(jnp.transpose(solved, (2, 1, 0)), 1), 2).astype(jnp.float32)
    edged = jnp.pad(pressure, ((1, 1), (0, 0), (0, 0)), mode='edge')
    edged = jnp.pad(edged, ((0, 0), (1, 1), (0, 0)), mode='wrap')
    grad_px, grad_py, grad_pz = central(edged)
    new_velocity = velocity - jnp.stack([grad_px, grad_py, grad_pz], 0)
    return (jnp.concatenate([new_velocity, predicted[3:5]], 0), pressure)
```

```python
import functools
import math

import jax
import jax.numpy as jnp
import ml_dtypes
import numpy as np
from jax import lax
from jax.experimental import pallas as pl
from jax.experimental.pallas import tpu as pltpu
from jax.sharding import PartitionSpec as P

EPSILON = 1e-06
STEP = 0.05
GRAVITY = 0.5
MOLECULAR = [0.02, 0.02, 0.02, 0.028, 0.04]
TURBULENT = [1.0, 1.0, 1.0, 1.0 / 0.85, 1.0 / 0.7]
PAIRS = [(0, 0), (1, 1), (2, 2), (0, 1), (0, 2), (1, 2)]
LANES = 128
SUBS = 8
CY = 3
ZB = 8


def basis(count):
    half = count // 2
    modes = np.arange(count)
    wave = np.where(modes <= half, modes, modes - half)
    phase = (wave[:, None] * np.arange(count)[None, :]) % count
    angle = 2.0 * math.pi / count * phase
    table = np.where(modes[:, None] <= half, np.cos(angle), np.sin(angle))
    weight = np.where((modes == 0) | (modes == half), 1.0, 2.0) / count
    lam = 2.0 - 2.0 * np.cos(2.0 * math.pi / count * wave)
    return table, weight, lam


def split_table(table):
    high = table.astype(ml_dtypes.bfloat16)
    low = (table - high.astype(np.float64)).astype(ml_dtypes.bfloat16)
    return high, low


@functools.lru_cache
def tables(length_x, span_all, wide, narrow):
    basis_x, weight_x, lam_x = basis(length_x)
    basis_z, weight_z, lam_z = basis(span_all)
    forward = split_table(basis_x.T)
    inverse = split_table(basis_x)
    rows = np.zeros((2 * narrow + 2 * wide, LANES), np.float32)
    rows[0:narrow] = lam_x.reshape(narrow, LANES)
    rows[narrow : 2 * narrow] = weight_x.reshape(narrow, LANES)
    rows[2 * narrow : 2 * narrow + wide] = lam_z[:, None]
    rows[2 * narrow + wide :] = weight_z[:, None]
    zmat = np.zeros((span_all, 512), np.float32)
    zmat[:, 0:span_all] = basis_z
    zmat[:, 128 : 128 + span_all] = basis_z.T
    for n in range(narrow):
        for y in range(CY):
            for side in range(2):
                z = (ZB * n - 1 if side == 0 else ZB * n + ZB) % span_all
                row = ZB * n + 2 * y + side
                zmat[row, 256 + y * span_all : 256 + (y + 1) * span_all] = basis_z[:, z]
    return (*forward, *inverse, rows, zmat)


def shift_x(value, step):
    lane = lax.broadcasted_iota(jnp.int32, value.shape, value.ndim - 1)
    if step > 0:
        moved = pltpu.roll(value, LANES - step, value.ndim - 1)
        carried = pltpu.roll(moved, SUBS - 1, value.ndim - 2)
        return jnp.where(lane >= LANES - step, carried, moved)
    moved = pltpu.roll(value, -step, value.ndim - 1)
    carried = pltpu.roll(moved, 1, value.ndim - 2)
    return jnp.where(lane < -step, carried, moved)


def three(below, centre, above):
    return (below + above) + (centre + centre)


def filter_x(value):
    return three(shift_x(value, -1), value, shift_x(value, 1)) * (1.0 / 64.0)


def strain(at, y, z):
    grads = []
    for i in range(3):
        here = at(i, y, z)
        grads.append(
            (
                shift_x(here, 1) - shift_x(here, -1),
                at(i, y + 1, z) - at(i, y - 1, z),
                at(i, y, z + 1) - at(i, y, z - 1),
            )
        )
    parts = [
        grads[i][i] if i == j else 0.5 * (grads[i][j] + grads[j][i]) for i, j in PAIRS
    ]
    diag = parts[0] * parts[0] + parts[1] * parts[1] + parts[2] * parts[2]
    off = parts[3] * parts[3] + parts[4] * parts[4] + parts[5] * parts[5]
    return parts, jnp.sqrt(0.5 * diag + off)


def shift_rows(value, step, filler):
    pad = jnp.full((abs(step), value.shape[1]), filler, value.dtype)
    if step > 0:
        return jnp.concatenate([pad, value[: value.shape[0] - step]], 0)
    return jnp.concatenate([value[-step:], pad], 0)


def exact_dot(left, right):
    return jnp.dot(
        left, right, precision=lax.Precision.HIGHEST, preferred_element_type=jnp.float32
    )


def split_dot(rows, high_ref, low_ref):
    count = rows.shape[0]
    high = rows.astype(jnp.bfloat16)
    low = (rows - high.astype(jnp.float32)).astype(jnp.bfloat16)
    both = jnp.dot(
        jnp.concatenate([high, low], 0), high_ref[...], preferred_element_type=jnp.float32
    )
    rest = jnp.dot(high, low_ref[...], preferred_element_type=jnp.float32)
    return both[:count] + (both[count:] + rest)


def kernel(
    wide,
    narrow,
    fields_hbm,
    bands_ref,
    fhigh_hbm,
    flow_hbm,
    ihigh_hbm,
    ilow_hbm,
    rows_hbm,
    zmat_hbm,
    out_ref,
    press_ref,
    nat,
    fhigh,
    flow,
    ihigh,
    ilow,
    rowtab,
    zmat,
    pad,
    yfilt,
    ymod,
    yprod,
    mag,
    filt,
    part_a,
    part_b,
    pred,
    div,
    sums,
    mine,
    factors,
    final,
    n_send,
    n_recv,
    w_send,
    w_recv,
    v_send,
    v_recv,
    u_send,
    u_recv,
    local_sem,
    halo_send,
    halo_recv,
    phase_send,
    phase_recv,
):
    w = lax.axis_index("wide")
    n = lax.axis_index("narrow")
    height = wide * CY
    w_down, w_up = lax.rem(w + wide - 1, wide), lax.rem(w + 1, wide)
    n_down, n_up = lax.rem(n + narrow - 1, narrow), lax.rem(n + 1, narrow)

    locals_ = [
        pltpu.make_async_copy(src, dst, local_sem.at[k])
        for k, (src, dst) in enumerate(
            [
                (fields_hbm, nat),
                (rows_hbm, rowtab),
                (zmat_hbm, zmat),
                (fhigh_hbm, fhigh),
                (flow_hbm, flow),
                (ihigh_hbm, ihigh),
                (ilow_hbm, ilow),
            ]
        )
    ]
    for copy in locals_:
        copy.start()

    barrier = pltpu.get_barrier_semaphore()

    def greet(to_w, to_n):
        pl.semaphore_signal(
            barrier,
            inc=1,
            device_id={"wide": to_w, "narrow": to_n},
            device_id_type=pl.DeviceIdType.MESH,
        )

    def greet_wide(d, carry):
        greet(lax.rem(w + d, wide), n)
        return carry

    for d in range(1, narrow):
        to_n = lax.rem(n + d, narrow)
        greet(w_down, to_n)
        greet(w_up, to_n)
        greet(w, to_n)
    lax.fori_loop(1, wide, greet_wide, 0)

    def remote(src, dst, send, recv, to_w, to_n):
        return pltpu.make_async_remote_copy(
            src_ref=src,
            dst_ref=dst,
            send_sem=send,
            recv_sem=recv,
            device_id={"wide": to_w, "narrow": to_n},
            device_id_type=pl.DeviceIdType.MESH,
        )

    locals_[0].wait()

    def to_tiles(f, carry):
        for y in range(CY):
            for z in range(ZB):
                pad[f, y + 3, z + 3] = nat[pl.ds((f * CY + y) * 64 + z, SUBS, stride=ZB), :]
        return carry

    lax.fori_loop(0, 5, to_tiles, 0)

    pl.semaphore_wait(barrier, (wide - 1) + 3 * (narrow - 1))

    def both(fs, ys, zs):
        return pad.at[pl.ds(*fs), pl.ds(*ys), pl.ds(*zs)]

    own_z = (3, ZB)
    own_y = (3, CY)
    vel, sca = (0, 3), (3, 2)
    plan = [
        (vel, (3, 2), own_z, (6, 2), own_z, w_down, n),
        (vel, (4, 2), own_z, (1, 2), own_z, w_up, n),
        (vel, (3, 2), (3, 2), (6, 2), (11, 2), w_down, n_down),
        (vel, (3, 2), (9, 2), (6, 2), (1, 2), w_down, n_up),
        (vel, (4, 2), (3, 2), (1, 2), (11, 2), w_up, n_down),
        (vel, (4, 2), (9, 2), (1, 2), (1, 2), w_up, n_up),
        (vel, own_y, (3, 2), own_y, (11, 2), w, n_down),
        (vel, own_y, (9, 2), own_y, (1, 2), w, n_up),
        (sca, (3, 2), own_z, (6, 2), own_z, w_down, n),
        (sca, (4, 2), own_z, (1, 2), own_z, w_up, n),
        (sca, own_y, (3, 2), own_y, (11, 2), w, n_down),
        (sca, own_y, (9, 2), own_y, (1, 2), w, n_up),
        ((1, 1), (5, 1), own_z, (8, 1), own_z, w_down, n),
        ((1, 1), (3, 1), own_z, (0, 1), own_z, w_up, n),
        ((2, 1), own_y, (5, 1), own_y, (13, 1), w, n_down),
        ((2, 1), own_y, (8, 1), own_y, (0, 1), w, n_up),
    ]
    halos = []
    for k, (fs, sy, sz, ty, tz, to_w, to_n) in enumerate(plan):
        halos.append(
            remote(
                both(fs, sy, sz), both(fs, ty, tz), halo_send.at[k], halo_recv.at[k], to_w, to_n
            )
        )
        halos[-1].start()

    locals_[1].wait()
    band = lax.broadcasted_iota(jnp.int32, (3, LANES), 0)
    spread = [
        lax.dot_general(
            bands_ref[...],
            jnp.where(band == k, 1.0, 0.0).astype(jnp.float32),
            (((0,), (0,)), ((), ())),
            precision=lax.Precision.HIGHEST,
            preferred_element_type=jnp.float32,
        )
        for k in range(3)
    ]
    eig = rowtab[pl.ds(n, 1), :] + rowtab[pl.ds(2 * narrow + w, 1), :]
    lower, diag, upper = spread[0], spread[1] + eig, spread[2]
    stride = 1
    level = 0
    while stride < height:
        inv = 1.0 / diag
        low = -lower * shift_rows(inv, stride, 1.0)
        high = -upper * shift_rows(inv, -stride, 1.0)
        factors[level, 0] = low
        factors[level, 1] = high
        diag = (
            diag
            + low * shift_rows(upper, stride, 0.0)
            + high * shift_rows(lower, -stride, 0.0)
        )
        lower = low * shift_rows(lower, stride, 0.0)
        upper = high * shift_rows(upper, -stride, 0.0)
        stride *= 2
        level += 1
    weight = rowtab[pl.ds(narrow + n, 1), :] * rowtab[pl.ds(2 * narrow + wide + w, 1), :]
    final[...] = -weight / diag

    for k in range(8):
        halos[k].wait_recv()

    def clear(start, fields, first):
        def one(z, carry):
            for f in range(fields[0], fields[0] + fields[1]):
                for y in range(first, first + start):
                    pad[f, y, z] = jnp.zeros((SUBS, LANES), jnp.float32)
            return carry

        lax.fori_loop(0, ZB + 6, one, 0)

    @pl.when(w == 0)
    def _():
        clear(2, vel, 1)

    @pl.when(w == wide - 1)
    def _():
        clear(2, vel, 6)

    def at_pad(f, y, z):
        return pad[f, y + 3, z + 3]

    def filter_rows(iz, carry):
        z = iz - 2
        for i in range(3):
            column = [at_pad(i, y, z) for y in range(-2, 5)]
            for y in range(5):
                yfilt[i, y, iz] = three(column[y], column[y + 1], column[y + 2])
        return carry

    lax.fori_loop(0, ZB + 4, filter_rows, 0)

    def local_terms(iz, carry):
        z = iz - 1
        modeled = []
        for y in range(-1, 4):
            parts, size = strain(at_pad, y, z)
            mag[y + 1, iz] = size
            modeled.append([size * part for part in parts])
        for p in range(6):
            for y in range(CY):
                ymod[p, y, iz] = three(modeled[y][p], modeled[y + 1][p], modeled[y + 2][p])
        columns = [[at_pad(i, y, z) for y in range(-1, 4)] for i in range(3)]
        for p, (i, j) in enumerate(PAIRS):
            prods = [columns[i][y] * columns[j][y] for y in range(5)]
            for y in range(CY):
                yprod[p, y, iz] = three(prods[y], prods[y + 1], prods[y + 2])
        for i in range(3):
            for y in range(5):
                value = three(yfilt[i, y, iz], yfilt[i, y, iz + 1], yfilt[i, y, iz + 2])
                filt[i, y, iz] = filter_x(value)
        return carry

    lax.fori_loop(0, ZB + 2, local_terms, 0)

    def at_filt(f, y, z):
        return filt[f, y + 1, z + 1]

    def plane_terms(z, carry):
        cross, square = list(carry[0]), list(carry[1])
        for y in range(CY):
            parts, size = strain(at_filt, y, z)
            centre = [at_filt(i, y, z) for i in range(3)]
            four = 4.0 * size
            lm_diag = lm_off = mm_diag = mm_off = None
            for p, (i, j) in enumerate(PAIRS):
                model = filter_x(three(ymod[p, y, z], ymod[p, y, z + 1], ymod[p, y, z + 2]))
                model = model - four * parts[p]
                stress = filter_x(three(yprod[p, y, z], yprod[p, y, z + 1], yprod[p, y, z + 2]))
                stress = stress - centre[i] * centre[j]
                if p < 3:
                    lm_diag = stress * model if lm_diag is None else lm_diag + stress * model
                    mm_diag = model * model if mm_diag is None else mm_diag + model * model
                else:
                    lm_off = stress * model if lm_off is None else lm_off + stress * model
                    mm_off = model * model if mm_off is None else mm_off + model * model
            cross[y] = cross[y] + (lm_diag + (lm_off + lm_off))
            square[y] = square[y] + (mm_diag + (mm_off + mm_off))
        return tuple(cross), tuple(square)

    nothing = jnp.zeros((SUBS, LANES), jnp.float32)
    cross, square = lax.fori_loop(
        0, ZB, plane_terms, ((nothing,) * CY, (nothing,) * CY)
    )
    packed = [jnp.sum(v, 0, keepdims=True) for v in (*cross, *square)]
    packed.append(jnp.zeros((SUBS - 2 * CY, LANES), jnp.float32))
    tile = jnp.concatenate(packed, 0)
    tile = jnp.broadcast_to(jnp.sum(tile, 1, keepdims=True), (SUBS, LANES))
    mine[...] = tile
    sums[pl.ds(narrow + n, 1)] = tile[None]
    peers = [(w_down, 2), (w, 1), (w_up, 0)]
    for d in range(narrow):
        to_n = lax.rem(n + d, narrow)
        for to_w, slot in peers:
            if d == 0 and slot == 1:
                continue
            remote(
                mine,
                sums.at[slot * narrow + n],
                phase_send.at[0],
                phase_recv.at[0],
                to_w,
                to_n,
            ).start()

    for k in range(8, 16):
        halos[k].wait_recv()

    @pl.when(w == 0)
    def _():
        clear(2, sca, 1)
        clear(1, (1, 1), 0)

    @pl.when(w == wide - 1)
    def _():
        clear(2, sca, 6)
        clear(1, (1, 1), 8)

    def slot_of(f, y, z):
        return pl.ds(pl.multiple_of(((f * 5 + y + 1) * (ZB + 2) + z + 1) * SUBS, SUBS), SUBS)

    def advance(fs, y, z):
        velocity = [at_pad(i, y, z) for i in range(3)]
        size = mag[y + 1, z + 1]
        for f in fs:
            here = velocity[f] if f < 3 else at_pad(f, y, z)
            xp, xm = shift_x(here, 1), shift_x(here, -1)
            yp, ym = at_pad(f, y + 1, z), at_pad(f, y - 1, z)
            zp, zm = at_pad(f, y, z + 1), at_pad(f, y, z - 1)
            ex = 8.0 * (xp - xm) - (shift_x(here, 2) - shift_x(here, -2))
            ey = 8.0 * (yp - ym) - (at_pad(f, y + 2, z) - at_pad(f, y - 2, z))
            ez = 8.0 * (zp - zm) - (at_pad(f, y, z + 2) - at_pad(f, y, z - 2))
            carried = velocity[0] * ex + velocity[1] * ey + velocity[2] * ez
            lap = ((xp + xm) + (yp + ym)) + ((zp + zm) - 6.0 * here)
            value = here - (STEP / 12.0) * carried + (STEP * MOLECULAR[f]) * lap
            if f == 1:
                value = value + (STEP * GRAVITY) * at_pad(3, y, z)
            part_a[slot_of(f, y, z), :] = value
            part_b[slot_of(f, y, z), :] = (STEP * TURBULENT[f]) * (size * lap)

    def advance_cells(z, carry):
        for y in range(CY):
            advance(range(5), y, z)
        advance((1,), -1, z)
        advance((1,), CY, z)
        return carry

    lax.fori_loop(0, ZB, advance_cells, 0)
    for y in range(CY):
        advance((2,), y, -1)
        advance((2,), y, ZB)

    pltpu.make_async_copy(
        sums.at[pl.ds(0, 3 * narrow - 1)], sums.at[pl.ds(0, 3 * narrow - 1)], phase_recv.at[0]
    ).wait()
    coef = []
    for slot, rows in ((0, (2,)), (1, (0, 1, 2)), (2, (0,))):
        total = sums[slot * narrow]
        for k in range(1, narrow):
            total = total + sums[slot * narrow + k]
        for row in rows:
            ratio = total[row : row + 1] / (total[CY + row : CY + row + 1] + EPSILON)
            coef.append(jnp.broadcast_to(ratio, (SUBS, LANES)))

    def finish(f, y, z, scale=None):
        value = part_a[slot_of(f, y, z), :] + coef[y + 1] * part_b[slot_of(f, y, z), :]
        pred[slot_of(f, y, z), :] = value if scale is None else value * scale

    inside_low = jnp.where(w == 0, 0.0, 1.0)
    inside_high = jnp.where(w == wide - 1, 0.0, 1.0)

    def finish_cells(z, carry):
        for y in range(CY):
            for f in range(5):
                finish(f, y, z)
        finish(1, -1, z, inside_low)
        finish(1, CY, z, inside_high)
        return carry

    lax.fori_loop(0, ZB, finish_cells, 0)
    for y in range(CY):
        finish(2, y, -1)
        finish(2, y, ZB)

    def at_pred(f, y, z):
        return pred[slot_of(f, y, z), :]

    def divergence(z, carry):
        for y in range(CY):
            stream = at_pred(0, y, z)
            value = shift_x(stream, 1) - shift_x(stream, -1)
            value = value + (at_pred(1, y + 1, z) - at_pred(1, y - 1, z))
            value = value + (at_pred(2, y, z + 1) - at_pred(2, y, z - 1))
            div[pl.ds(pl.multiple_of((y * ZB + z) * SUBS, SUBS), SUBS), :] = 0.5 * value
        return carry

    lax.fori_loop(0, ZB, divergence, 0)

    locals_[3].wait()
    locals_[4].wait()
    flat = jnp.concatenate(
        [div[pl.ds(s, CY * ZB, stride=SUBS), :] for s in range(SUBS)], 1
    )
    flat = jnp.concatenate([flat, jnp.zeros((8, flat.shape[1]), jnp.float32)], 0)
    spectrum = split_dot(flat, fhigh, flow)
    for k in range(narrow):
        for y in range(CY):
            n_send[k, :, LANES * y : LANES * (y + 1)] = spectrum[
                ZB * y : ZB * (y + 1), LANES * k : LANES * (k + 1)
            ]

    def exchange_narrow(source, target, phase):
        for d in range(1, narrow):
            to_n = lax.rem(n + d, narrow)
            remote(
                source.at[to_n], target.at[n], phase_send.at[phase], phase_recv.at[phase], w, to_n
            ).start()
        target[pl.ds(n, 1)] = source[pl.ds(n, 1)]
        pltpu.make_async_copy(
            target.at[pl.ds(0, narrow - 1)],
            target.at[pl.ds(0, narrow - 1)],
            phase_recv.at[phase],
        ).wait()

    exchange_narrow(n_send, n_recv, 1)
    locals_[2].wait()
    spanwise = exact_dot(
        zmat[:, 0:wide], n_recv[...].reshape(narrow * ZB, CY * LANES)
    )
    for y in range(CY):
        w_send[:, y] = spanwise[:, LANES * y : LANES * (y + 1)].reshape(wide, 1, LANES)

    def post_forward(d, carry):
        to_w = lax.rem(w + d, wide)
        remote(
            w_send.at[to_w], w_recv.at[w], phase_send.at[2], phase_recv.at[2], to_w, n
        ).start()
        return carry

    lax.fori_loop(1, wide, post_forward, 0)
    w_recv[pl.ds(w, 1)] = w_send[pl.ds(w, 1)]
    pltpu.make_async_copy(
        w_recv.at[pl.ds(0, wide - 1)], w_recv.at[pl.ds(0, wide - 1)], phase_recv.at[2]
    ).wait()

    rhs = w_recv[...].reshape(height, LANES)
    stride = 1
    level = 0
    while stride < height:
        rhs = (
            rhs
            + factors[level, 0] * shift_rows(rhs, stride, 0.0)
            + factors[level, 1] * shift_rows(rhs, -stride, 0.0)
        )
        stride *= 2
        level += 1
    phi = rhs * final[...]
    v_send[pl.ds(1, height)] = phi.reshape(height, 1, LANES)
    v_send[0] = phi[0:1]
    v_send[height + 1] = phi[height - 1 : height]

    def post_backward(d, carry):
        to_w = lax.rem(w + d, wide)
        remote(
            v_send.at[pl.ds(CY * to_w, CY + 2)],
            v_recv.at[w],
            phase_send.at[3],
            phase_recv.at[3],
            to_w,
            n,
        ).start()
        return carry

    lax.fori_loop(1, wide, post_backward, 0)
    v_recv[pl.ds(w, 1)] = v_send[pl.ds(CY * w, CY + 2)].reshape(1, CY + 2, 1, LANES)
    pltpu.make_async_copy(
        v_recv.at[pl.ds(0, wide - 1)], v_recv.at[pl.ds(0, wide - 1)], phase_recv.at[3]
    ).wait()

    planes = [v_recv[:, k].reshape(wide, LANES) for k in range(CY + 2)]
    cells = exact_dot(zmat[:, 128 : 128 + wide], jnp.concatenate(planes, 1))
    rims = exact_dot(
        zmat[:, 256 : 256 + CY * wide], jnp.concatenate(planes[1 : CY + 1], 0)
    )
    for k in range(narrow):
        u_send[k, :, 0 : (CY + 2) * LANES] = cells[ZB * k : ZB * (k + 1)]
        u_send[k, :, (CY + 2) * LANES :] = rims[ZB * k : ZB * (k + 1)]
    exchange_narrow(u_send, u_recv, 4)

    locals_[5].wait()
    locals_[6].wait()
    rows = [
        jnp.concatenate(
            [u_recv[k, :, LANES * r : LANES * (r + 1)] for k in range(narrow)], 1
        )
        for r in range(CY + 3)
    ]
    potential = split_dot(jnp.concatenate(rows, 0), ihigh, ilow)
    length_x = potential.shape[1]
    rim = potential[(CY + 2) * ZB :]
    row_id = lax.broadcasted_iota(jnp.int32, (ZB, length_x), 0)

    for y in range(CY):
        here = potential[(y + 1) * ZB : (y + 2) * ZB]
        below = potential[y * ZB : (y + 1) * ZB]
        above = potential[(y + 2) * ZB : (y + 3) * ZB]
        press_ref[y] = here
        left = jnp.where(row_id == 0, rim[2 * y : 2 * y + 1], pltpu.roll(here, 1, 0))
        right = jnp.where(
            row_id == ZB - 1, rim[2 * y + 1 : 2 * y + 2], pltpu.roll(here, ZB - 1, 0)
        )
        grads = [
            pltpu.roll(here, length_x - 1, 1) - pltpu.roll(here, 1, 1),
            above - below,
            right - left,
        ]
        for f in range(5):
            for s in range(SUBS):
                first = ((f * 5 + y + 1) * (ZB + 2) + 1) * SUBS + s
                value = pred[pl.ds(first, ZB, stride=SUBS), :]
                lanes = slice(LANES * s, LANES * (s + 1))
                if f < 3:
                    value = value - 0.5 * grads[f][:, lanes]
                out_ref[f, y, :, lanes] = value

    for halo in halos:
        halo.wait_send()
    part = sums.at[pl.ds(0, 3 * narrow - 1)]
    pltpu.make_async_copy(part, part, phase_send.at[0]).wait()
    for phase, ref in ((1, n_send), (4, u_send)):
        part = ref.at[pl.ds(0, narrow - 1)]
        pltpu.make_async_copy(part, part, phase_send.at[phase]).wait()
    for phase, ref in ((2, w_recv), (3, v_recv)):
        part = ref.at[pl.ds(0, wide - 1)]
        pltpu.make_async_copy(part, part, phase_send.at[phase]).wait()


def body(wide, narrow, consts, fields, y_bands):
    span_here, length_x = fields.shape[2], fields.shape[3]
    tiled = fields.reshape(5, CY, span_here, SUBS, LANES).transpose(0, 1, 3, 2, 4)
    tiled = tiled.reshape(5 * CY * SUBS * span_here, LANES)
    f32 = jnp.float32
    levels = math.ceil(math.log2(wide * CY))
    points = 5 * 5 * (ZB + 2) * SUBS
    vmem = pltpu.VMEM
    scratch = [
        vmem(tiled.shape, f32),
        *[vmem((length_x, length_x), jnp.bfloat16) for _ in range(4)],
        vmem(consts[4].shape, f32),
        vmem(consts[5].shape, f32),
        vmem((5, CY + 6, ZB + 6, SUBS, LANES), f32),
        vmem((3, CY + 2, ZB + 4, SUBS, LANES), f32),
        vmem((6, CY, ZB + 2, SUBS, LANES), f32),
        vmem((6, CY, ZB + 2, SUBS, LANES), f32),
        vmem((CY + 2, ZB + 2, SUBS, LANES), f32),
        vmem((3, CY + 2, ZB + 2, SUBS, LANES), f32),
        vmem((points, LANES), f32),
        vmem((points, LANES), f32),
        vmem((points, LANES), f32),
        vmem((CY * ZB * SUBS, LANES), f32),
        vmem((3 * narrow, SUBS, LANES), f32),
        vmem((SUBS, LANES), f32),
        vmem((levels, 2, wide * CY, LANES), f32),
        vmem((wide * CY, LANES), f32),
        vmem((narrow, ZB, CY * LANES), f32),
        vmem((narrow, ZB, CY * LANES), f32),
        vmem((wide, CY, 1, LANES), f32),
        vmem((wide, CY, 1, LANES), f32),
        vmem((wide * CY + 2, 1, LANES), f32),
        vmem((wide, CY + 2, 1, LANES), f32),
        vmem((narrow, ZB, (CY + 3) * LANES), f32),
        vmem((narrow, ZB, (CY + 3) * LANES), f32),
        pltpu.SemaphoreType.DMA((7,)),
        pltpu.SemaphoreType.DMA((16,)),
        pltpu.SemaphoreType.DMA((16,)),
        pltpu.SemaphoreType.DMA((5,)),
        pltpu.SemaphoreType.DMA((5,)),
    ]
    hbm = pl.BlockSpec(memory_space=pltpu.HBM)
    inside = pl.BlockSpec(memory_space=pltpu.VMEM)
    return pl.pallas_call(
        functools.partial(kernel, wide, narrow),
        out_shape=(
            jax.ShapeDtypeStruct(fields.shape, f32),
            jax.ShapeDtypeStruct(fields.shape[1:], f32),
        ),
        in_specs=[hbm, inside, *[hbm] * 6],
        out_specs=(inside, inside),
        scratch_shapes=scratch,
        compiler_params=pltpu.CompilerParams(
            collective_id=0, has_side_effects=True, vmem_limit_bytes=48 * 1024 * 1024
        ),
    )(tiled, y_bands, *consts)


def solution(mesh):
    wide, narrow = mesh.shape["wide"], mesh.shape["narrow"]

    def run(fields, y_bands):
        consts = tables(fields.shape[3], fields.shape[2], wide, narrow)
        consts = [jnp.asarray(table) for table in consts]
        return jax.shard_map(
            functools.partial(body, wide, narrow, consts),
            mesh=mesh,
            in_specs=(P(None, "wide", "narrow", None), P()),
            out_specs=(P(None, "wide", "narrow", None), P("wide", "narrow", None)),
            check_vma=False,
        )(fields, y_bands)

    return run
```

```python
import functools
import math

import jax
import jax.numpy as jnp
import ml_dtypes
import numpy as np
from jax import lax
from jax.experimental import pallas as pl
from jax.experimental.pallas import tpu as pltpu
from jax.sharding import PartitionSpec as P

EPSILON = 1e-06
STEP = 0.05
GRAVITY = 0.5
MOLECULAR = [0.02, 0.02, 0.02, 0.028, 0.04]
TURBULENT = [1.0, 1.0, 1.0, 1.0 / 0.85, 1.0 / 0.7]
PAIRS = [(0, 0), (1, 1), (2, 2), (0, 1), (0, 2), (1, 2)]
LANES = 128
SUBS = 8
CY = 3
ZB = 8


def basis(count):
    half = count // 2
    modes = np.arange(count)
    wave = np.where(modes <= half, modes, modes - half)
    phase = (wave[:, None] * np.arange(count)[None, :]) % count
    angle = 2.0 * math.pi / count * phase
    table = np.where(modes[:, None] <= half, np.cos(angle), np.sin(angle))
    weight = np.where((modes == 0) | (modes == half), 1.0, 2.0) / count
    lam = 2.0 - 2.0 * np.cos(2.0 * math.pi / count * wave)
    return table, weight, lam


def split_table(table):
    high = table.astype(ml_dtypes.bfloat16)
    low = (table - high.astype(np.float64)).astype(ml_dtypes.bfloat16)
    return high, low


@functools.lru_cache
def tables(length_x, span_all, wide, narrow):
    basis_x, weight_x, lam_x = basis(length_x)
    basis_z, weight_z, lam_z = basis(span_all)
    forward = split_table(basis_x.T)
    inverse = split_table(basis_x)
    rows = np.zeros((2 * narrow + 2 * wide, LANES), np.float32)
    rows[0:narrow] = lam_x.reshape(narrow, LANES)
    rows[narrow : 2 * narrow] = weight_x.reshape(narrow, LANES)
    rows[2 * narrow : 2 * narrow + wide] = lam_z[:, None]
    rows[2 * narrow + wide :] = weight_z[:, None]
    zmat = np.zeros((span_all, 512), np.float32)
    zmat[:, 0:span_all] = basis_z
    zmat[:, 128 : 128 + span_all] = basis_z.T
    for n in range(narrow):
        for y in range(CY):
            for side in range(2):
                z = (ZB * n - 1 if side == 0 else ZB * n + ZB) % span_all
                row = ZB * n + 2 * y + side
                zmat[row, 256 + y * span_all : 256 + (y + 1) * span_all] = basis_z[:, z]
    return (*forward, *inverse, rows, zmat)


def shift_x(value, step):
    lane = lax.broadcasted_iota(jnp.int32, value.shape, value.ndim - 1)
    if step > 0:
        moved = pltpu.roll(value, LANES - step, value.ndim - 1)
        carried = pltpu.roll(moved, SUBS - 1, value.ndim - 2)
        return jnp.where(lane >= LANES - step, carried, moved)
    moved = pltpu.roll(value, -step, value.ndim - 1)
    carried = pltpu.roll(moved, 1, value.ndim - 2)
    return jnp.where(lane < -step, carried, moved)


def three(below, centre, above):
    return (below + above) + (centre + centre)


def filter_x(value):
    return three(shift_x(value, -1), value, shift_x(value, 1)) * (1.0 / 64.0)


def strain(at, y, z):
    grads = []
    for i in range(3):
        here = at(i, y, z)
        grads.append(
            (
                shift_x(here, 1) - shift_x(here, -1),
                at(i, y + 1, z) - at(i, y - 1, z),
                at(i, y, z + 1) - at(i, y, z - 1),
            )
        )
    parts = [
        grads[i][i] if i == j else 0.5 * (grads[i][j] + grads[j][i]) for i, j in PAIRS
    ]
    diag = parts[0] * parts[0] + parts[1] * parts[1] + parts[2] * parts[2]
    off = parts[3] * parts[3] + parts[4] * parts[4] + parts[5] * parts[5]
    return parts, jnp.sqrt(0.5 * diag + off)


def shift_rows(value, step, filler):
    pad = jnp.full((abs(step), value.shape[1]), filler, value.dtype)
    if step > 0:
        return jnp.concatenate([pad, value[: value.shape[0] - step]], 0)
    return jnp.concatenate([value[-step:], pad], 0)


def exact_dot(left, right):
    return jnp.dot(
        left, right, precision=lax.Precision.HIGHEST, preferred_element_type=jnp.float32
    )


def split_dot(rows, high_ref, low_ref):
    count = rows.shape[0]
    high = rows.astype(jnp.bfloat16)
    low = (rows - high.astype(jnp.float32)).astype(jnp.bfloat16)
    both = jnp.dot(
        jnp.concatenate([high, low], 0), high_ref[...], preferred_element_type=jnp.float32
    )
    rest = jnp.dot(high, low_ref[...], preferred_element_type=jnp.float32)
    return both[:count] + (both[count:] + rest)


def kernel(
    wide,
    narrow,
    fields_hbm,
    bands_ref,
    fhigh_hbm,
    flow_hbm,
    ihigh_hbm,
    ilow_hbm,
    rows_hbm,
    zmat_hbm,
    out_ref,
    press_ref,
    nat,
    fhigh,
    flow,
    ihigh,
    ilow,
    rowtab,
    zmat,
    pad,
    yfilt,
    ymod,
    yprod,
    mag,
    filt,
    part_a,
    part_b,
    pred,
    div,
    sums,
    mine,
    factors,
    final,
    n_send,
    n_recv,
    w_send,
    w_recv,
    v_send,
    v_recv,
    u_send,
    u_recv,
    local_sem,
    round_sem,
    halo_send,
    halo_recv,
    phase_send,
    phase_recv,
):
    w = lax.axis_index("wide")
    n = lax.axis_index("narrow")
    height = wide * CY
    w_down, w_up = lax.rem(w + wide - 1, wide), lax.rem(w + 1, wide)
    n_down, n_up = lax.rem(n + narrow - 1, narrow), lax.rem(n + 1, narrow)

    locals_ = [
        pltpu.make_async_copy(src, dst, local_sem.at[k])
        for k, (src, dst) in enumerate(
            [
                (fields_hbm, nat),
                (rows_hbm, rowtab),
                (zmat_hbm, zmat),
                (fhigh_hbm, fhigh),
                (flow_hbm, flow),
                (ihigh_hbm, ihigh),
                (ilow_hbm, ilow),
            ]
        )
    ]
    for copy in locals_:
        copy.start()

    barrier = pltpu.get_barrier_semaphore()

    def greet(to_w, to_n):
        pl.semaphore_signal(
            barrier,
            inc=1,
            device_id={"wide": to_w, "narrow": to_n},
            device_id_type=pl.DeviceIdType.MESH,
        )

    for d in range(1, narrow):
        to_n = lax.rem(n + d, narrow)
        greet(w_down, to_n)
        greet(w_up, to_n)
        greet(w, to_n)
    greet(w_up, n)
    rounds = [1 << r for r in range(wide.bit_length() - 1)]
    for reach in rounds:
        greet(lax.rem(w + wide - reach, wide), n)

    def tell(r):
        pl.semaphore_signal(
            round_sem.at[r],
            inc=1,
            device_id={"wide": lax.rem(w + rounds[r], wide), "narrow": n},
            device_id_type=pl.DeviceIdType.MESH,
        )

    def hear(r):
        pl.semaphore_wait(round_sem.at[r], 1)

    def remote(src, dst, send, recv, to_w, to_n):
        return pltpu.make_async_remote_copy(
            src_ref=src,
            dst_ref=dst,
            send_sem=send,
            recv_sem=recv,
            device_id={"wide": to_w, "narrow": to_n},
            device_id_type=pl.DeviceIdType.MESH,
        )

    locals_[0].wait()

    def to_tiles(f, carry):
        for y in range(CY):
            for z in range(ZB):
                pad[f, y + 3, z + 3] = nat[pl.ds((f * CY + y) * 64 + z, SUBS, stride=ZB), :]
        return carry

    lax.fori_loop(0, 5, to_tiles, 0)
    for f in range(3):
        for y in (1, 7):
            for z in (1, 12):
                pad[f, y, z] = jnp.zeros((SUBS, LANES), jnp.float32)

    pl.semaphore_wait(barrier, 3 * (narrow - 1) + 1 + len(rounds))

    def both(fs, ys, zs):
        return pad.at[pl.ds(*fs), pl.ds(*ys), pl.ds(*zs)]

    own_z = (3, ZB)
    own_y = (3, CY)
    vel, sca = (0, 3), (3, 2)
    first = [
        (vel, (3, 2), own_z, (6, 2), own_z, w_down, n),
        (vel, (4, 2), own_z, (1, 2), own_z, w_up, n),
        (vel, (3, 1), (3, 2), (6, 1), (11, 2), w_down, n_down),
        (vel, (3, 1), (9, 2), (6, 1), (1, 2), w_down, n_up),
        (vel, (5, 1), (3, 2), (2, 1), (11, 2), w_up, n_down),
        (vel, (5, 1), (9, 2), (2, 1), (1, 2), w_up, n_up),
        (vel, (4, 1), (3, 1), (7, 1), (11, 1), w_down, n_down),
        (vel, (4, 1), (10, 1), (7, 1), (2, 1), w_down, n_up),
        (vel, (4, 1), (3, 1), (1, 1), (11, 1), w_up, n_down),
        (vel, (4, 1), (10, 1), (1, 1), (2, 1), w_up, n_up),
        (vel, own_y, (3, 2), own_y, (11, 2), w, n_down),
        (vel, own_y, (9, 2), own_y, (1, 2), w, n_up),
    ]
    second = [
        ((1, 1), (5, 1), own_z, (8, 1), own_z, w_down, n),
        ((1, 1), (3, 1), own_z, (0, 1), own_z, w_up, n),
        ((3, 1), (3, 1), own_z, (6, 1), own_z, w_down, n),
        ((3, 1), (5, 1), own_z, (2, 1), own_z, w_up, n),
        ((2, 1), own_y, (5, 1), own_y, (13, 1), w, n_down),
        ((2, 1), own_y, (8, 1), own_y, (0, 1), w, n_up),
    ]
    third = [
        ((3, 1), (4, 1), own_z, (7, 1), own_z, w_down, n),
        ((3, 1), (4, 1), own_z, (1, 1), own_z, w_up, n),
        ((4, 1), (3, 2), own_z, (6, 2), own_z, w_down, n),
        ((4, 1), (4, 2), own_z, (1, 2), own_z, w_up, n),
        (sca, own_y, (3, 2), own_y, (11, 2), w, n_down),
        (sca, own_y, (9, 2), own_y, (1, 2), w, n_up),
    ]
    halos = [
        remote(both(fs, sy, sz), both(fs, ty, tz), halo_send.at[k], halo_recv.at[k], to_w, to_n)
        for k, (fs, sy, sz, ty, tz, to_w, to_n) in enumerate(first + second + third)
    ]
    cut_a, cut_b = len(first), len(first) + len(second)
    for halo in halos[:cut_a]:
        halo.start()
    tell(0)

    locals_[1].wait()
    band = lax.broadcasted_iota(jnp.int32, (3, LANES), 0)
    spread = [
        lax.dot_general(
            bands_ref[...],
            jnp.where(band == k, 1.0, 0.0).astype(jnp.float32),
            (((0,), (0,)), ((), ())),
            precision=lax.Precision.HIGHEST,
            preferred_element_type=jnp.float32,
        )
        for k in range(3)
    ]
    eig = rowtab[pl.ds(n, 1), :] + rowtab[pl.ds(2 * narrow + w, 1), :]
    lower, diag, upper = spread[0], spread[1] + eig, spread[2]
    stride = 1
    level = 0
    while stride < height:
        inv = 1.0 / diag
        low = -lower * shift_rows(inv, stride, 1.0)
        high = -upper * shift_rows(inv, -stride, 1.0)
        factors[level, 0] = low
        factors[level, 1] = high
        diag = (
            diag
            + low * shift_rows(upper, stride, 0.0)
            + high * shift_rows(lower, -stride, 0.0)
        )
        lower = low * shift_rows(lower, stride, 0.0)
        upper = high * shift_rows(upper, -stride, 0.0)
        stride *= 2
        level += 1
    weight = rowtab[pl.ds(narrow + n, 1), :] * rowtab[pl.ds(2 * narrow + wide + w, 1), :]
    final[...] = -weight / diag

    hear(0)
    tell(1)
    for halo in halos[:cut_a]:
        halo.wait_send()
    for halo in halos[cut_a:]:
        halo.start()
    hear(1)
    tell(2)
    for halo in halos[:cut_a]:
        halo.wait_recv()
    hear(2)
    tell(3)

    def clear(start, fields, first):
        def one(z, carry):
            for f in range(fields[0], fields[0] + fields[1]):
                for y in range(first, first + start):
                    pad[f, y, z] = jnp.zeros((SUBS, LANES), jnp.float32)
            return carry

        lax.fori_loop(0, ZB + 6, one, 0)

    @pl.when(w == 0)
    def _():
        clear(2, vel, 1)

    @pl.when(w == wide - 1)
    def _():
        clear(2, vel, 6)

    def at_pad(f, y, z):
        return pad[f, y + 3, z + 3]

    def filter_rows(iz, carry):
        z = iz - 2
        for i in range(3):
            column = [at_pad(i, y, z) for y in range(-2, 5)]
            for y in range(5):
                yfilt[i, y, iz] = three(column[y], column[y + 1], column[y + 2])
        return carry

    lax.fori_loop(0, ZB + 4, filter_rows, 0)

    def local_terms(iz, carry):
        z = iz - 1
        modeled = []
        for y in range(-1, 4):
            parts, size = strain(at_pad, y, z)
            mag[y + 1, iz] = size
            modeled.append([size * part for part in parts])
        for p in range(6):
            for y in range(CY):
                ymod[p, y, iz] = three(modeled[y][p], modeled[y + 1][p], modeled[y + 2][p])
        columns = [[at_pad(i, y, z) for y in range(-1, 4)] for i in range(3)]
        for p, (i, j) in enumerate(PAIRS):
            prods = [columns[i][y] * columns[j][y] for y in range(5)]
            for y in range(CY):
                yprod[p, y, iz] = three(prods[y], prods[y + 1], prods[y + 2])
        for i in range(3):
            for y in range(5):
                value = three(yfilt[i, y, iz], yfilt[i, y, iz + 1], yfilt[i, y, iz + 2])
                filt[i, y, iz] = filter_x(value)
        return carry

    lax.fori_loop(0, ZB + 2, local_terms, 0)

    def at_filt(f, y, z):
        return filt[f, y + 1, z + 1]

    def plane_terms(z, carry):
        cross, square = list(carry[0]), list(carry[1])
        for y in range(CY):
            parts, size = strain(at_filt, y, z)
            centre = [at_filt(i, y, z) for i in range(3)]
            four = 4.0 * size
            lm_diag = lm_off = mm_diag = mm_off = None
            for p, (i, j) in enumerate(PAIRS):
                model = filter_x(three(ymod[p, y, z], ymod[p, y, z + 1], ymod[p, y, z + 2]))
                model = model - four * parts[p]
                stress = filter_x(three(yprod[p, y, z], yprod[p, y, z + 1], yprod[p, y, z + 2]))
                stress = stress - centre[i] * centre[j]
                if p < 3:
                    lm_diag = stress * model if lm_diag is None else lm_diag + stress * model
                    mm_diag = model * model if mm_diag is None else mm_diag + model * model
                else:
                    lm_off = stress * model if lm_off is None else lm_off + stress * model
                    mm_off = model * model if mm_off is None else mm_off + model * model
            cross[y] = cross[y] + (lm_diag + (lm_off + lm_off))
            square[y] = square[y] + (mm_diag + (mm_off + mm_off))
        return tuple(cross), tuple(square)

    nothing = jnp.zeros((SUBS, LANES), jnp.float32)
    cross, square = lax.fori_loop(
        0, ZB, plane_terms, ((nothing,) * CY, (nothing,) * CY)
    )
    packed = [jnp.sum(v, 0, keepdims=True) for v in (*cross, *square)]
    packed.append(jnp.zeros((SUBS - 2 * CY, LANES), jnp.float32))
    tile = jnp.concatenate(packed, 0)
    tile = jnp.broadcast_to(jnp.sum(tile, 1, keepdims=True), (SUBS, LANES))
    mine[...] = tile
    sums[pl.ds(narrow + n, 1)] = tile[None]
    half_n = narrow // 2
    side_n, cell_n = lax.div(n, half_n), lax.rem(n, half_n)
    others = []
    for d_side, d_cell in ((1, 2), (1, 1), (1, 3), (0, 2), (1, 0), (0, 1), (0, 3)):
        others.append(
            lax.rem(side_n + d_side, 2) * half_n + lax.rem(cell_n + d_cell, half_n)
        )
    peers = [(w_down, 2), (w_up, 0), (w, 1)]
    for to_n in (*others, n):
        for to_w, slot in peers:
            if to_n is n and slot == 1:
                continue
            remote(
                mine,
                sums.at[slot * narrow + n],
                phase_send.at[0],
                phase_recv.at[0],
                to_w,
                to_n,
            ).start()

    hear(3)
    tell(4)
    for halo in halos[cut_a:cut_b]:
        halo.wait_recv()

    @pl.when(w == 0)
    def _():
        clear(1, (3, 1), 2)
        clear(1, (1, 1), 0)

    @pl.when(w == wide - 1)
    def _():
        clear(1, (3, 1), 6)
        clear(1, (1, 1), 8)

    def slot_of(f, y, z):
        return pl.ds(pl.multiple_of(((f * 5 + y + 1) * (ZB + 2) + z + 1) * SUBS, SUBS), SUBS)

    def advance(fs, y, z):
        velocity = [at_pad(i, y, z) for i in range(3)]
        size = mag[y + 1, z + 1]
        for f in fs:
            here = velocity[f] if f < 3 else at_pad(f, y, z)
            xp, xm = shift_x(here, 1), shift_x(here, -1)
            yp, ym = at_pad(f, y + 1, z), at_pad(f, y - 1, z)
            zp, zm = at_pad(f, y, z + 1), at_pad(f, y, z - 1)
            ex = 8.0 * (xp - xm) - (shift_x(here, 2) - shift_x(here, -2))
            ey = 8.0 * (yp - ym) - (at_pad(f, y + 2, z) - at_pad(f, y - 2, z))
            ez = 8.0 * (zp - zm) - (at_pad(f, y, z + 2) - at_pad(f, y, z - 2))
            carried = velocity[0] * ex + velocity[1] * ey + velocity[2] * ez
            lap = ((xp + xm) + (yp + ym)) + ((zp + zm) - 6.0 * here)
            value = here - (STEP / 12.0) * carried + (STEP * MOLECULAR[f]) * lap
            if f == 1:
                value = value + (STEP * GRAVITY) * at_pad(3, y, z)
            part_a[slot_of(f, y, z), :] = value
            part_b[slot_of(f, y, z), :] = (STEP * TURBULENT[f]) * (size * lap)

    def advance_cells(z, carry):
        for y in range(CY):
            advance(range(3), y, z)
        advance((1,), -1, z)
        advance((1,), CY, z)
        return carry

    lax.fori_loop(0, ZB, advance_cells, 0)
    for y in range(CY):
        advance((2,), y, -1)
        advance((2,), y, ZB)

    hear(4)
    tell(5)
    pltpu.make_async_copy(
        sums.at[pl.ds(0, 3 * narrow - 1)], sums.at[pl.ds(0, 3 * narrow - 1)], phase_recv.at[0]
    ).wait()
    coef = []
    for slot, rows in ((0, (2,)), (1, (0, 1, 2)), (2, (0,))):
        total = sums[slot * narrow]
        for k in range(1, narrow):
            total = total + sums[slot * narrow + k]
        for row in rows:
            ratio = total[row : row + 1] / (total[CY + row : CY + row + 1] + EPSILON)
            coef.append(jnp.broadcast_to(ratio, (SUBS, LANES)))

    def finish(f, y, z, scale=None):
        value = part_a[slot_of(f, y, z), :] + coef[y + 1] * part_b[slot_of(f, y, z), :]
        pred[slot_of(f, y, z), :] = value if scale is None else value * scale

    inside_low = jnp.where(w == 0, 0.0, 1.0)
    inside_high = jnp.where(w == wide - 1, 0.0, 1.0)

    def finish_cells(z, carry):
        for y in range(CY):
            for f in range(3):
                finish(f, y, z)
        finish(1, -1, z, inside_low)
        finish(1, CY, z, inside_high)
        return carry

    lax.fori_loop(0, ZB, finish_cells, 0)
    for y in range(CY):
        finish(2, y, -1)
        finish(2, y, ZB)

    def at_pred(f, y, z):
        return pred[slot_of(f, y, z), :]

    def divergence(z, carry):
        for y in range(CY):
            stream = at_pred(0, y, z)
            value = shift_x(stream, 1) - shift_x(stream, -1)
            value = value + (at_pred(1, y + 1, z) - at_pred(1, y - 1, z))
            value = value + (at_pred(2, y, z + 1) - at_pred(2, y, z - 1))
            div[pl.ds(pl.multiple_of((y * ZB + z) * SUBS, SUBS), SUBS), :] = 0.5 * value
        return carry

    lax.fori_loop(0, ZB, divergence, 0)

    locals_[3].wait()
    locals_[4].wait()
    flat = jnp.concatenate(
        [div[pl.ds(s, CY * ZB, stride=SUBS), :] for s in range(SUBS)], 1
    )
    flat = jnp.concatenate([flat, jnp.zeros((8, flat.shape[1]), jnp.float32)], 0)
    spectrum = split_dot(flat, fhigh, flow)
    for k in range(narrow):
        for y in range(CY):
            n_send[k, :, LANES * y : LANES * (y + 1)] = spectrum[
                ZB * y : ZB * (y + 1), LANES * k : LANES * (k + 1)
            ]

    def exchange_narrow(source, target, phase):
        for to_n in others:
            remote(
                source.at[to_n], target.at[n], phase_send.at[phase], phase_recv.at[phase], w, to_n
            ).start()
        target[pl.ds(n, 1)] = source[pl.ds(n, 1)]
        pltpu.make_async_copy(
            target.at[pl.ds(0, narrow - 1)],
            target.at[pl.ds(0, narrow - 1)],
            phase_recv.at[phase],
        ).wait()

    exchange_narrow(n_send, n_recv, 1)
    locals_[2].wait()
    spanwise = exact_dot(
        zmat[:, 0:wide], n_recv[...].reshape(narrow * ZB, CY * LANES)
    )
    for y in range(CY):
        w_send[:, y] = spanwise[:, LANES * y : LANES * (y + 1)].reshape(wide, 1, LANES)

    depth = wide // 8
    w_z, w_y, w_c = lax.div(w, 8), lax.rem(lax.div(w, 2), 4), lax.rem(w, 2)

    def swing(k):
        return lax.div(k, 2) * (1 - 2 * lax.rem(k, 2)) - lax.rem(k, 2)

    def partner(k):
        to_z = lax.rem(w_z + depth // 2 + swing(lax.div(k, 8)) + depth, depth)
        to_y = lax.rem(w_y + 2 + swing(lax.rem(lax.div(k, 2), 4)) + 4, 4)
        to_c = lax.rem(w_c + 1 - lax.rem(k, 2), 2)
        return (to_z * 4 + to_y) * 2 + to_c

    def post_forward(k, carry):
        to_w = partner(k)
        remote(
            w_send.at[to_w], w_recv.at[w], phase_send.at[2], phase_recv.at[2], to_w, n
        ).start()
        return carry

    hear(5)
    lax.fori_loop(0, wide - 1, post_forward, 0)
    w_recv[pl.ds(w, 1)] = w_send[pl.ds(w, 1)]

    for halo in halos[cut_b:]:
        halo.wait_recv()

    @pl.when(w == 0)
    def _():
        clear(2, sca, 1)

    @pl.when(w == wide - 1)
    def _():
        clear(2, sca, 6)

    def scalar_cells(z, carry):
        for y in range(CY):
            advance((3, 4), y, z)
            for f in (3, 4):
                finish(f, y, z)
        return carry

    lax.fori_loop(0, ZB, scalar_cells, 0)

    def to_rows(f, carry):
        for y in range(CY):
            for s in range(SUBS):
                start = ((f * 5 + y + 1) * (ZB + 2) + 1) * SUBS + s
                out_ref[f, y, :, LANES * s : LANES * (s + 1)] = pred[
                    pl.ds(start, ZB, stride=SUBS), :
                ]
        return carry

    lax.fori_loop(0, 5, to_rows, 0)
    pltpu.make_async_copy(
        w_recv.at[pl.ds(0, wide - 1)], w_recv.at[pl.ds(0, wide - 1)], phase_recv.at[2]
    ).wait()

    rhs = w_recv[...].reshape(height, LANES)
    stride = 1
    level = 0
    while stride < height:
        rhs = (
            rhs
            + factors[level, 0] * shift_rows(rhs, stride, 0.0)
            + factors[level, 1] * shift_rows(rhs, -stride, 0.0)
        )
        stride *= 2
        level += 1
    phi = rhs * final[...]
    v_send[pl.ds(1, height)] = phi.reshape(height, 1, LANES)
    v_send[0] = phi[0:1]
    v_send[height + 1] = phi[height - 1 : height]

    def post_backward(k, carry):
        to_w = partner(k)
        remote(
            v_send.at[pl.ds(CY * to_w, CY + 2)],
            v_recv.at[w],
            phase_send.at[3],
            phase_recv.at[3],
            to_w,
            n,
        ).start()
        return carry

    lax.fori_loop(0, wide - 1, post_backward, 0)
    v_recv[pl.ds(w, 1)] = v_send[pl.ds(CY * w, CY + 2)].reshape(1, CY + 2, 1, LANES)
    pltpu.make_async_copy(
        v_recv.at[pl.ds(0, wide - 1)], v_recv.at[pl.ds(0, wide - 1)], phase_recv.at[3]
    ).wait()

    planes = [v_recv[:, k].reshape(wide, LANES) for k in range(CY + 2)]
    cells = exact_dot(zmat[:, 128 : 128 + wide], jnp.concatenate(planes, 1))
    rims = exact_dot(
        zmat[:, 256 : 256 + CY * wide], jnp.concatenate(planes[1 : CY + 1], 0)
    )
    for k in range(narrow):
        u_send[k, :, 0 : (CY + 2) * LANES] = cells[ZB * k : ZB * (k + 1)]
        u_send[k, :, (CY + 2) * LANES :] = rims[ZB * k : ZB * (k + 1)]
    exchange_narrow(u_send, u_recv, 4)

    locals_[5].wait()
    locals_[6].wait()
    rows = [
        jnp.concatenate(
            [u_recv[k, :, LANES * r : LANES * (r + 1)] for k in range(narrow)], 1
        )
        for r in range(CY + 3)
    ]
    potential = split_dot(jnp.concatenate(rows, 0), ihigh, ilow)
    length_x = potential.shape[1]
    rim = potential[(CY + 2) * ZB :]
    row_id = lax.broadcasted_iota(jnp.int32, (ZB, length_x), 0)

    for y in range(CY):
        here = potential[(y + 1) * ZB : (y + 2) * ZB]
        below = potential[y * ZB : (y + 1) * ZB]
        above = potential[(y + 2) * ZB : (y + 3) * ZB]
        press_ref[y] = here
        left = jnp.where(row_id == 0, rim[2 * y : 2 * y + 1], pltpu.roll(here, 1, 0))
        right = jnp.where(
            row_id == ZB - 1, rim[2 * y + 1 : 2 * y + 2], pltpu.roll(here, ZB - 1, 0)
        )
        grads = [
            pltpu.roll(here, length_x - 1, 1) - pltpu.roll(here, 1, 1),
            above - below,
            right - left,
        ]
        for f in range(3):
            out_ref[f, y] = out_ref[f, y] - 0.5 * grads[f]

    for halo in halos[cut_a:]:
        halo.wait_send()
    part = sums.at[pl.ds(0, 3 * narrow - 1)]
    pltpu.make_async_copy(part, part, phase_send.at[0]).wait()
    for phase, ref in ((1, n_send), (4, u_send)):
        part = ref.at[pl.ds(0, narrow - 1)]
        pltpu.make_async_copy(part, part, phase_send.at[phase]).wait()
    for phase, ref in ((2, w_recv), (3, v_recv)):
        part = ref.at[pl.ds(0, wide - 1)]
        pltpu.make_async_copy(part, part, phase_send.at[phase]).wait()


def body(wide, narrow, consts, fields, y_bands):
    span_here, length_x = fields.shape[2], fields.shape[3]
    tiled = fields.reshape(5, CY, span_here, SUBS, LANES).transpose(0, 1, 3, 2, 4)
    tiled = tiled.reshape(5 * CY * SUBS * span_here, LANES)
    f32 = jnp.float32
    levels = math.ceil(math.log2(wide * CY))
    points = 5 * 5 * (ZB + 2) * SUBS
    vmem = pltpu.VMEM
    scratch = [
        vmem(tiled.shape, f32),
        *[vmem((length_x, length_x), jnp.bfloat16) for _ in range(4)],
        vmem(consts[4].shape, f32),
        vmem(consts[5].shape, f32),
        vmem((5, CY + 6, ZB + 6, SUBS, LANES), f32),
        vmem((3, CY + 2, ZB + 4, SUBS, LANES), f32),
        vmem((6, CY, ZB + 2, SUBS, LANES), f32),
        vmem((6, CY, ZB + 2, SUBS, LANES), f32),
        vmem((CY + 2, ZB + 2, SUBS, LANES), f32),
        vmem((3, CY + 2, ZB + 2, SUBS, LANES), f32),
        vmem((points, LANES), f32),
        vmem((points, LANES), f32),
        vmem((points, LANES), f32),
        vmem((CY * ZB * SUBS, LANES), f32),
        vmem((3 * narrow, SUBS, LANES), f32),
        vmem((SUBS, LANES), f32),
        vmem((levels, 2, wide * CY, LANES), f32),
        vmem((wide * CY, LANES), f32),
        vmem((narrow, ZB, CY * LANES), f32),
        vmem((narrow, ZB, CY * LANES), f32),
        vmem((wide, CY, 1, LANES), f32),
        vmem((wide, CY, 1, LANES), f32),
        vmem((wide * CY + 2, 1, LANES), f32),
        vmem((wide, CY + 2, 1, LANES), f32),
        vmem((narrow, ZB, (CY + 3) * LANES), f32),
        vmem((narrow, ZB, (CY + 3) * LANES), f32),
        pltpu.SemaphoreType.DMA((7,)),
        pltpu.SemaphoreType.REGULAR((wide.bit_length() - 1,)),
        pltpu.SemaphoreType.DMA((24,)),
        pltpu.SemaphoreType.DMA((24,)),
        pltpu.SemaphoreType.DMA((5,)),
        pltpu.SemaphoreType.DMA((5,)),
    ]
    hbm = pl.BlockSpec(memory_space=pltpu.HBM)
    inside = pl.BlockSpec(memory_space=pltpu.VMEM)
    return pl.pallas_call(
        functools.partial(kernel, wide, narrow),
        out_shape=(
            jax.ShapeDtypeStruct(fields.shape, f32),
            jax.ShapeDtypeStruct(fields.shape[1:], f32),
        ),
        in_specs=[hbm, inside, *[hbm] * 6],
        out_specs=(inside, inside),
        scratch_shapes=scratch,
        compiler_params=pltpu.CompilerParams(
            collective_id=0, has_side_effects=True, vmem_limit_bytes=61 * 1024 * 1024
        ),
    )(tiled, y_bands, *consts)


def solution(mesh):
    wide, narrow = mesh.shape["wide"], mesh.shape["narrow"]

    def run(fields, y_bands):
        consts = tables(fields.shape[3], fields.shape[2], wide, narrow)
        consts = [jnp.asarray(table) for table in consts]
        return jax.shard_map(
            functools.partial(body, wide, narrow, consts),
            mesh=mesh,
            in_specs=(P(None, "wide", "narrow", None), P()),
            out_specs=(P(None, "wide", "narrow", None), P("wide", "narrow", None)),
            check_vma=False,
        )(fields, y_bands)

    return run
```

```python
import functools
import math

import jax
import jax.numpy as jnp
import ml_dtypes
import numpy as np
from jax import lax
from jax.experimental import pallas as pl
from jax.experimental.pallas import tpu as pltpu
from jax.sharding import PartitionSpec as P

EPSILON = 1e-06
STEP = 0.05
GRAVITY = 0.5
MOLECULAR = [0.02, 0.02, 0.02, 0.028, 0.04]
TURBULENT = [1.0, 1.0, 1.0, 1.0 / 0.85, 1.0 / 0.7]
PAIRS = [(0, 0), (1, 1), (2, 2), (0, 1), (0, 2), (1, 2)]
LANES = 128
SUBS = 8
CY = 3
ZB = 8


def basis(count):
    half = count // 2
    modes = np.arange(count)
    wave = np.where(modes <= half, modes, modes - half)
    phase = (wave[:, None] * np.arange(count)[None, :]) % count
    angle = 2.0 * math.pi / count * phase
    table = np.where(modes[:, None] <= half, np.cos(angle), np.sin(angle))
    weight = np.where((modes == 0) | (modes == half), 1.0, 2.0) / count
    lam = 2.0 - 2.0 * np.cos(2.0 * math.pi / count * wave)
    return table, weight, lam


def split_table(table):
    high = table.astype(ml_dtypes.bfloat16)
    low = (table - high.astype(np.float64)).astype(ml_dtypes.bfloat16)
    return high, low


@functools.lru_cache
def tables(length_x, span_all, wide, narrow):
    basis_x, weight_x, lam_x = basis(length_x)
    basis_z, weight_z, lam_z = basis(span_all)
    forward = split_table(basis_x.T)
    inverse = split_table(basis_x)
    rows = np.zeros((2 * narrow + 2 * wide, LANES), np.float32)
    rows[0:narrow] = lam_x.reshape(narrow, LANES)
    rows[narrow : 2 * narrow] = weight_x.reshape(narrow, LANES)
    rows[2 * narrow : 2 * narrow + wide] = lam_z[:, None]
    rows[2 * narrow + wide :] = weight_z[:, None]
    zmat = np.zeros((span_all, 512), np.float32)
    zmat[:, 0:span_all] = basis_z
    zmat[:, 128 : 128 + span_all] = basis_z.T
    for n in range(narrow):
        for y in range(CY):
            for side in range(2):
                z = (ZB * n - 1 if side == 0 else ZB * n + ZB) % span_all
                row = ZB * n + 2 * y + side
                zmat[row, 256 + y * span_all : 256 + (y + 1) * span_all] = basis_z[:, z]
    small = np.zeros((length_x, length_x), np.float32)
    small[0 : rows.shape[0], 0:LANES] = rows
    small[0:span_all, LANES : LANES + 512] = zmat
    return (*forward, *inverse, small)


def shift_x(value, step):
    lane = lax.broadcasted_iota(jnp.int32, value.shape, value.ndim - 1)
    if step > 0:
        moved = pltpu.roll(value, LANES - step, value.ndim - 1)
        carried = pltpu.roll(moved, SUBS - 1, value.ndim - 2)
        return jnp.where(lane >= LANES - step, carried, moved)
    moved = pltpu.roll(value, -step, value.ndim - 1)
    carried = pltpu.roll(moved, 1, value.ndim - 2)
    return jnp.where(lane < -step, carried, moved)


def three(below, centre, above):
    return (below + above) + (centre + centre)


def filter_x(value):
    return three(shift_x(value, -1), value, shift_x(value, 1)) * (1.0 / 64.0)


def strain(at, y, z):
    grads = []
    for i in range(3):
        here = at(i, y, z)
        grads.append(
            (
                shift_x(here, 1) - shift_x(here, -1),
                at(i, y + 1, z) - at(i, y - 1, z),
                at(i, y, z + 1) - at(i, y, z - 1),
            )
        )
    parts = [
        grads[i][i] if i == j else 0.5 * (grads[i][j] + grads[j][i]) for i, j in PAIRS
    ]
    diag = parts[0] * parts[0] + parts[1] * parts[1] + parts[2] * parts[2]
    off = parts[3] * parts[3] + parts[4] * parts[4] + parts[5] * parts[5]
    return parts, jnp.sqrt(0.5 * diag + off)


def shift_rows(value, step, filler):
    pad = jnp.full((abs(step), value.shape[1]), filler, value.dtype)
    if step > 0:
        return jnp.concatenate([pad, value[: value.shape[0] - step]], 0)
    return jnp.concatenate([value[-step:], pad], 0)


def exact_dot(left, right):
    return jnp.dot(
        left, right, precision=lax.Precision.HIGHEST, preferred_element_type=jnp.float32
    )


def split_dot(rows, high_ref, low_ref):
    count = rows.shape[0]
    high = rows.astype(jnp.bfloat16)
    low = (rows - high.astype(jnp.float32)).astype(jnp.bfloat16)
    both = jnp.dot(
        jnp.concatenate([high, low], 0), high_ref[...], preferred_element_type=jnp.float32
    )
    rest = jnp.dot(high, low_ref[...], preferred_element_type=jnp.float32)
    return both[:count] + (both[count:] + rest)


def kernel(
    wide,
    narrow,
    fields_hbm,
    bands_ref,
    fhigh_hbm,
    flow_hbm,
    ihigh_hbm,
    ilow_hbm,
    small_hbm,
    out_ref,
    press_ref,
    nat,
    fhigh,
    flow,
    ihigh,
    ilow,
    rowtab,
    zmat,
    pad,
    yfilt,
    ymod,
    yprod,
    mag,
    filt,
    part_a,
    part_b,
    pred,
    div,
    sums,
    mine,
    bands,
    block,
    chain,
    factors,
    n_send,
    n_recv,
    w_send,
    w_recv,
    v_send,
    v_recv,
    u_send,
    u_recv,
    local_sem,
    round_sem,
    halo_send,
    halo_recv,
    phase_send,
    phase_recv,
):
    w = lax.axis_index("wide")
    n = lax.axis_index("narrow")
    w_down, w_up = lax.rem(w + wide - 1, wide), lax.rem(w + 1, wide)
    n_down, n_up = lax.rem(n + narrow - 1, narrow), lax.rem(n + 1, narrow)

    locals_ = [
        pltpu.make_async_copy(src, dst, local_sem.at[k])
        for k, (src, dst) in enumerate(
            [
                (fields_hbm, nat),
                (small_hbm.at[pl.ds(0, rowtab.shape[0]), pl.ds(0, LANES)], rowtab),
                (small_hbm.at[pl.ds(0, zmat.shape[0]), pl.ds(LANES, 512)], zmat),
                (fhigh_hbm, fhigh),
                (flow_hbm, flow),
                (ihigh_hbm, ihigh),
                (ilow_hbm, ilow),
            ]
        )
    ]
    for copy in locals_:
        copy.start()

    barrier = pltpu.get_barrier_semaphore()

    def greet(to_w, to_n):
        pl.semaphore_signal(
            barrier,
            inc=1,
            device_id={"wide": to_w, "narrow": to_n},
            device_id_type=pl.DeviceIdType.MESH,
        )

    for d in range(1, narrow):
        to_n = lax.rem(n + d, narrow)
        greet(w_down, to_n)
        greet(w_up, to_n)
        greet(w, to_n)
    greet(w_up, n)
    rounds = [1 << r for r in range(wide.bit_length() - 1)]
    for reach in rounds:
        greet(lax.rem(w + wide - reach, wide), n)

    def tell(r):
        pl.semaphore_signal(
            round_sem.at[r],
            inc=1,
            device_id={"wide": lax.rem(w + rounds[r], wide), "narrow": n},
            device_id_type=pl.DeviceIdType.MESH,
        )

    def hear(r):
        pl.semaphore_wait(round_sem.at[r], 1)

    def remote(src, dst, send, recv, to_w, to_n):
        return pltpu.make_async_remote_copy(
            src_ref=src,
            dst_ref=dst,
            send_sem=send,
            recv_sem=recv,
            device_id={"wide": to_w, "narrow": to_n},
            device_id_type=pl.DeviceIdType.MESH,
        )

    locals_[0].wait()

    def to_tiles(f, carry):
        for y in range(CY):
            for z in range(ZB):
                pad[f, y + 3, z + 3] = nat[pl.ds((f * CY + y) * 64 + z, SUBS, stride=ZB), :]
        return carry

    lax.fori_loop(0, 5, to_tiles, 0)
    for f in range(3):
        for y in (1, 7):
            for z in (1, 12):
                pad[f, y, z] = jnp.zeros((SUBS, LANES), jnp.float32)

    pl.semaphore_wait(barrier, 3 * (narrow - 1) + 1 + len(rounds))

    def both(fs, ys, zs):
        return pad.at[pl.ds(*fs), pl.ds(*ys), pl.ds(*zs)]

    own_z = (3, ZB)
    own_y = (3, CY)
    vel, sca = (0, 3), (3, 2)
    first = [
        (vel, (3, 2), own_z, (6, 2), own_z, w_down, n),
        (vel, (4, 2), own_z, (1, 2), own_z, w_up, n),
        (vel, (3, 1), (3, 2), (6, 1), (11, 2), w_down, n_down),
        (vel, (3, 1), (9, 2), (6, 1), (1, 2), w_down, n_up),
        (vel, (5, 1), (3, 2), (2, 1), (11, 2), w_up, n_down),
        (vel, (5, 1), (9, 2), (2, 1), (1, 2), w_up, n_up),
        (vel, (4, 1), (3, 1), (7, 1), (11, 1), w_down, n_down),
        (vel, (4, 1), (10, 1), (7, 1), (2, 1), w_down, n_up),
        (vel, (4, 1), (3, 1), (1, 1), (11, 1), w_up, n_down),
        (vel, (4, 1), (10, 1), (1, 1), (2, 1), w_up, n_up),
        (vel, own_y, (3, 2), own_y, (11, 2), w, n_down),
        (vel, own_y, (9, 2), own_y, (1, 2), w, n_up),
    ]
    second = [
        ((1, 1), (5, 1), own_z, (8, 1), own_z, w_down, n),
        ((1, 1), (3, 1), own_z, (0, 1), own_z, w_up, n),
        ((3, 1), (3, 1), own_z, (6, 1), own_z, w_down, n),
        ((3, 1), (5, 1), own_z, (2, 1), own_z, w_up, n),
        ((2, 1), own_y, (5, 1), own_y, (13, 1), w, n_down),
        ((2, 1), own_y, (8, 1), own_y, (0, 1), w, n_up),
    ]
    third = [
        ((3, 1), (4, 1), own_z, (7, 1), own_z, w_down, n),
        ((3, 1), (4, 1), own_z, (1, 1), own_z, w_up, n),
        ((4, 1), (3, 2), own_z, (6, 2), own_z, w_down, n),
        ((4, 1), (4, 2), own_z, (1, 2), own_z, w_up, n),
        (sca, own_y, (3, 2), own_y, (11, 2), w, n_down),
        (sca, own_y, (9, 2), own_y, (1, 2), w, n_up),
    ]
    halos = [
        remote(both(fs, sy, sz), both(fs, ty, tz), halo_send.at[k], halo_recv.at[k], to_w, to_n)
        for k, (fs, sy, sz, ty, tz, to_w, to_n) in enumerate(first + second + third)
    ]
    cut_a, cut_b = len(first), len(first) + len(second)
    for halo in halos[:cut_a]:
        halo.start()
    tell(0)

    locals_[1].wait()
    band = lax.broadcasted_iota(jnp.int32, (3, LANES), 0)
    spread = [
        lax.dot_general(
            bands_ref[...],
            jnp.where(band == k, 1.0, 0.0).astype(jnp.float32),
            (((0,), (0,)), ((), ())),
            precision=lax.Precision.HIGHEST,
            preferred_element_type=jnp.float32,
        )
        for k in range(3)
    ]
    for k in range(3):
        bands[k] = spread[k]

    def invert(low, mid, high):
        det = 1.0 / (mid[0] * mid[1] - high[0] * low[1])
        return mid[1] * det, -high[0] * det, -low[1] * det, mid[0] * det

    lam_x = rowtab[pl.ds(n, 1), :]
    eig = rowtab[2 * narrow : 2 * narrow + wide, :] + lam_x
    own_low, own_mid, own_high = (
        [bands[k, pl.ds(CY * w + j, 1), :] for j in range(CY)] for k in range(3)
    )
    for k, part in enumerate(invert(own_low, [m + eig for m in own_mid[:2]], own_high)):
        block[k] = part
    block[4] = -rowtab[2 * narrow + wide :, :] * rowtab[pl.ds(narrow + n, 1), :]

    eig = lam_x + rowtab[pl.ds(2 * narrow + w, 1), :]
    low, mid, high = (
        [bands[k, pl.ds(j, wide, stride=CY), :] for j in range(CY)] for k in range(3)
    )
    mid = [m + eig for m in mid]
    i00, i01, i10, i11 = invert(low, mid, high)
    from_low, from_high = -i00 * low[0], -i01 * high[1]
    chain[0], chain[1], chain[2] = from_low, from_high, -high[2]
    lower = -low[2] * i10 * low[0]
    diag = mid[2] - low[2] * i11 * high[1] + high[2] * shift_rows(from_low, -1, 0.0)
    upper = high[2] * shift_rows(from_high, -1, 0.0)
    stride = 1
    level = 0
    while stride < wide:
        inv = 1.0 / diag
        to_low = -lower * shift_rows(inv, stride, 1.0)
        to_high = -upper * shift_rows(inv, -stride, 1.0)
        factors[level, 0] = to_low
        factors[level, 1] = to_high
        diag = (
            diag
            + to_low * shift_rows(upper, stride, 0.0)
            + to_high * shift_rows(lower, -stride, 0.0)
        )
        lower = to_low * shift_rows(lower, stride, 0.0)
        upper = to_high * shift_rows(upper, -stride, 0.0)
        stride *= 2
        level += 1
    chain[3] = 1.0 / diag

    hear(0)
    tell(1)
    for halo in halos[:cut_a]:
        halo.wait_send()
    for halo in halos[cut_a:]:
        halo.start()

    def clear(rows, fields, cells):
        def one(z, carry):
            for f in fields:
                for y in rows:
                    pad[f, y, z] = jnp.zeros((SUBS, LANES), jnp.float32)
            return carry

        lax.fori_loop(cells[0], cells[1], one, 0)

    def outside(below, above, fields, cells):
        @pl.when(w == 0)
        def _():
            for part in cells:
                clear(below, fields, part)

        @pl.when(w == wide - 1)
        def _():
            for part in cells:
                clear(above, fields, part)

    def at_pad(f, y, z):
        return pad[f, y + 3, z + 3]

    def filter_rows(iz, carry):
        z = iz - 2
        for i in range(3):
            column = [at_pad(i, y, z) for y in range(-2, 5)]
            for y in range(5):
                yfilt[i, y, iz] = three(column[y], column[y + 1], column[y + 2])
        return carry


    def local_terms(iz, carry):
        z = iz - 1
        modeled = []
        for y in range(-1, 4):
            parts, size = strain(at_pad, y, z)
            mag[y + 1, iz] = size
            modeled.append([size * part for part in parts])
        for p in range(6):
            for y in range(CY):
                ymod[p, y, iz] = three(modeled[y][p], modeled[y + 1][p], modeled[y + 2][p])
        columns = [[at_pad(i, y, z) for y in range(-1, 4)] for i in range(3)]
        for p, (i, j) in enumerate(PAIRS):
            prods = [columns[i][y] * columns[j][y] for y in range(5)]
            for y in range(CY):
                yprod[p, y, iz] = three(prods[y], prods[y + 1], prods[y + 2])
        for i in range(3):
            for y in range(5):
                value = three(yfilt[i, y, iz], yfilt[i, y, iz + 1], yfilt[i, y, iz + 2])
                filt[i, y, iz] = filter_x(value)
        return carry


    def at_filt(f, y, z):
        return filt[f, y + 1, z + 1]

    def plane_terms(z, carry):
        cross, square = list(carry[0]), list(carry[1])
        for y in range(CY):
            parts, size = strain(at_filt, y, z)
            centre = [at_filt(i, y, z) for i in range(3)]
            four = 4.0 * size
            lm_diag = lm_off = mm_diag = mm_off = None
            for p, (i, j) in enumerate(PAIRS):
                model = filter_x(three(ymod[p, y, z], ymod[p, y, z + 1], ymod[p, y, z + 2]))
                model = model - four * parts[p]
                stress = filter_x(three(yprod[p, y, z], yprod[p, y, z + 1], yprod[p, y, z + 2]))
                stress = stress - centre[i] * centre[j]
                if p < 3:
                    lm_diag = stress * model if lm_diag is None else lm_diag + stress * model
                    mm_diag = model * model if mm_diag is None else mm_diag + model * model
                else:
                    lm_off = stress * model if lm_off is None else lm_off + stress * model
                    mm_off = model * model if mm_off is None else mm_off + model * model
            cross[y] = cross[y] + (lm_diag + (lm_off + lm_off))
            square[y] = square[y] + (mm_diag + (mm_off + mm_off))
        return tuple(cross), tuple(square)

    nothing = jnp.zeros((SUBS, LANES), jnp.float32)
    plane = ((nothing,) * CY, (nothing,) * CY)

    def edges(step, inner):
        return lambda k, carry: step(k + lax.div(k, 2) * inner, carry)

    inner_cells, rim_cells = (3, ZB + 3), ((1, 3), (ZB + 3, ZB + 5))
    for halo in halos[:2]:
        halo.wait_recv()
    hear(1)
    tell(2)
    outside((1, 2), (6, 7), range(3), (inner_cells,))
    lax.fori_loop(2, ZB + 2, filter_rows, 0)
    lax.fori_loop(2, ZB, local_terms, 0)
    plane = lax.fori_loop(2, ZB - 2, plane_terms, plane)
    for halo in halos[2:cut_a]:
        halo.wait_recv()
    outside((1, 2), (6, 7), range(3), rim_cells)
    lax.fori_loop(0, 4, edges(filter_rows, ZB), 0)
    lax.fori_loop(0, 4, edges(local_terms, ZB - 2), 0)
    cross, square = lax.fori_loop(0, 4, edges(plane_terms, ZB - 4), plane)
    packed = [jnp.sum(v, 0, keepdims=True) for v in (*cross, *square)]
    packed.append(jnp.zeros((SUBS - 2 * CY, LANES), jnp.float32))
    tile = jnp.concatenate(packed, 0)
    tile = jnp.broadcast_to(jnp.sum(tile, 1, keepdims=True), (SUBS, LANES))
    mine[...] = tile
    sums[pl.ds(narrow + n, 1)] = tile[None]
    half_n = narrow // 2
    side_n, cell_n = lax.div(n, half_n), lax.rem(n, half_n)
    others = []
    for d_side, d_cell in ((1, 2), (1, 1), (1, 3), (0, 2), (1, 0), (0, 1), (0, 3)):
        others.append(
            lax.rem(side_n + d_side, 2) * half_n + lax.rem(cell_n + d_cell, half_n)
        )
    peers = [(w_down, 2), (w_up, 0), (w, 1)]
    for to_n in (*others, n):
        for to_w, slot in peers:
            if to_n is n and slot == 1:
                continue
            remote(
                mine,
                sums.at[slot * narrow + n],
                phase_send.at[0],
                phase_recv.at[0],
                to_w,
                to_n,
            ).start()

    hear(2)
    tell(3)
    for halo in halos[cut_a:cut_b]:
        halo.wait_recv()
    outside((2,), (6,), (3,), (inner_cells,))
    outside((0,), (8,), (1,), (inner_cells,))

    def slot_of(f, y, z):
        return pl.ds(pl.multiple_of(((f * 5 + y + 1) * (ZB + 2) + z + 1) * SUBS, SUBS), SUBS)

    def advance(fs, y, z):
        velocity = [at_pad(i, y, z) for i in range(3)]
        size = mag[y + 1, z + 1]
        for f in fs:
            here = velocity[f] if f < 3 else at_pad(f, y, z)
            xp, xm = shift_x(here, 1), shift_x(here, -1)
            yp, ym = at_pad(f, y + 1, z), at_pad(f, y - 1, z)
            zp, zm = at_pad(f, y, z + 1), at_pad(f, y, z - 1)
            ex = 8.0 * (xp - xm) - (shift_x(here, 2) - shift_x(here, -2))
            ey = 8.0 * (yp - ym) - (at_pad(f, y + 2, z) - at_pad(f, y - 2, z))
            ez = 8.0 * (zp - zm) - (at_pad(f, y, z + 2) - at_pad(f, y, z - 2))
            carried = velocity[0] * ex + velocity[1] * ey + velocity[2] * ez
            lap = ((xp + xm) + (yp + ym)) + ((zp + zm) - 6.0 * here)
            value = here - (STEP / 12.0) * carried + (STEP * MOLECULAR[f]) * lap
            if f == 1:
                value = value + (STEP * GRAVITY) * at_pad(3, y, z)
            part_a[slot_of(f, y, z), :] = value
            part_b[slot_of(f, y, z), :] = (STEP * TURBULENT[f]) * (size * lap)

    def advance_cells(z, carry):
        for y in range(CY):
            advance(range(3), y, z)
        advance((1,), -1, z)
        advance((1,), CY, z)
        return carry

    lax.fori_loop(0, ZB, advance_cells, 0)
    for y in range(CY):
        advance((2,), y, -1)
        advance((2,), y, ZB)

    hear(3)
    tell(4)
    pltpu.make_async_copy(
        sums.at[pl.ds(0, 3 * narrow - 1)], sums.at[pl.ds(0, 3 * narrow - 1)], phase_recv.at[0]
    ).wait()
    coef = []
    for slot, rows in ((0, (2,)), (1, (0, 1, 2)), (2, (0,))):
        total = sums[slot * narrow]
        for k in range(1, narrow):
            total = total + sums[slot * narrow + k]
        for row in rows:
            ratio = total[row : row + 1] / (total[CY + row : CY + row + 1] + EPSILON)
            coef.append(jnp.broadcast_to(ratio, (SUBS, LANES)))

    def finish(f, y, z, scale=None):
        value = part_a[slot_of(f, y, z), :] + coef[y + 1] * part_b[slot_of(f, y, z), :]
        pred[slot_of(f, y, z), :] = value if scale is None else value * scale

    inside_low = jnp.where(w == 0, 0.0, 1.0)
    inside_high = jnp.where(w == wide - 1, 0.0, 1.0)

    def finish_cells(z, carry):
        for y in range(CY):
            for f in range(3):
                finish(f, y, z)
        finish(1, -1, z, inside_low)
        finish(1, CY, z, inside_high)
        return carry

    lax.fori_loop(0, ZB, finish_cells, 0)
    for y in range(CY):
        finish(2, y, -1)
        finish(2, y, ZB)

    def at_pred(f, y, z):
        return pred[slot_of(f, y, z), :]

    def divergence(z, carry):
        for y in range(CY):
            stream = at_pred(0, y, z)
            value = shift_x(stream, 1) - shift_x(stream, -1)
            value = value + (at_pred(1, y + 1, z) - at_pred(1, y - 1, z))
            value = value + (at_pred(2, y, z + 1) - at_pred(2, y, z - 1))
            div[pl.ds(pl.multiple_of((y * ZB + z) * SUBS, SUBS), SUBS), :] = 0.5 * value
        return carry

    lax.fori_loop(0, ZB, divergence, 0)

    locals_[3].wait()
    locals_[4].wait()
    flat = jnp.concatenate(
        [div[pl.ds(s, CY * ZB, stride=SUBS), :] for s in range(SUBS)], 1
    )
    flat = jnp.concatenate([flat, jnp.zeros((8, flat.shape[1]), jnp.float32)], 0)
    spectrum = split_dot(flat, fhigh, flow)
    for k in range(narrow):
        for y in range(CY):
            n_send[k, :, LANES * y : LANES * (y + 1)] = spectrum[
                ZB * y : ZB * (y + 1), LANES * k : LANES * (k + 1)
            ]

    def exchange_narrow(source, target, phase):
        for to_n in others:
            remote(
                source.at[to_n], target.at[n], phase_send.at[phase], phase_recv.at[phase], w, to_n
            ).start()
        target[pl.ds(n, 1)] = source[pl.ds(n, 1)]
        pltpu.make_async_copy(
            target.at[pl.ds(0, narrow - 1)],
            target.at[pl.ds(0, narrow - 1)],
            phase_recv.at[phase],
        ).wait()

    hear(4)
    tell(5)
    exchange_narrow(n_send, n_recv, 1)
    locals_[2].wait()
    spanwise = exact_dot(
        zmat[:, 0:wide], n_recv[...].reshape(narrow * ZB, CY * LANES)
    )
    rhs = [spanwise[:, LANES * y : LANES * (y + 1)] * block[4] for y in range(CY)]
    inner_0 = block[0] * rhs[0] + block[1] * rhs[1]
    inner_1 = block[2] * rhs[0] + block[3] * rhs[1]
    w_send[:, 0] = inner_0.reshape(wide, 1, LANES)
    w_send[:, 1] = (rhs[2] - own_low[2] * inner_1).reshape(wide, 1, LANES)

    depth = wide // 8
    w_z, w_y, w_c = lax.div(w, 8), lax.rem(lax.div(w, 2), 4), lax.rem(w, 2)

    def swing(k):
        return lax.div(k, 2) * (1 - 2 * lax.rem(k, 2)) - lax.rem(k, 2)

    def partner(k):
        to_z = lax.rem(w_z + depth // 2 + swing(lax.div(k, 8)) + depth, depth)
        to_y = lax.rem(w_y + 2 + swing(lax.rem(lax.div(k, 2), 4)) + 4, 4)
        to_c = lax.rem(w_c + 1 - lax.rem(k, 2), 2)
        return (to_z * 4 + to_y) * 2 + to_c

    def post_forward(k, carry):
        to_w = partner(k)
        remote(
            w_send.at[to_w], w_recv.at[w], phase_send.at[2], phase_recv.at[2], to_w, n
        ).start()
        return carry

    hear(5)
    lax.fori_loop(0, wide - 1, post_forward, 0)
    w_recv[pl.ds(w, 1)] = w_send[pl.ds(w, 1)]

    for halo in halos[cut_b:]:
        halo.wait_recv()

    outside((1, 2), (6, 7), (3, 4), (inner_cells,))

    def scalar_cells(z, carry):
        for y in range(CY):
            advance((3, 4), y, z)
            for f in (3, 4):
                finish(f, y, z)
        return carry

    lax.fori_loop(0, ZB, scalar_cells, 0)

    def to_rows(f, carry):
        for y in range(CY):
            for s in range(SUBS):
                start = ((f * 5 + y + 1) * (ZB + 2) + 1) * SUBS + s
                out_ref[f, y, :, LANES * s : LANES * (s + 1)] = pred[
                    pl.ds(start, ZB, stride=SUBS), :
                ]
        return carry

    lax.fori_loop(0, 5, to_rows, 0)
    pltpu.make_async_copy(
        w_recv.at[pl.ds(0, wide - 1)], w_recv.at[pl.ds(0, wide - 1)], phase_recv.at[2]
    ).wait()

    first_row = w_recv[:, 0].reshape(wide, LANES)
    last = w_recv[:, 1].reshape(wide, LANES) + chain[2] * shift_rows(first_row, -1, 0.0)
    stride = 1
    level = 0
    while stride < wide:
        last = (
            last
            + factors[level, 0] * shift_rows(last, stride, 0.0)
            + factors[level, 1] * shift_rows(last, -stride, 0.0)
        )
        stride *= 2
        level += 1
    last = last * chain[3]
    before = shift_rows(last, 1, 0.0)
    first_row = first_row + chain[0] * before + chain[1] * last
    before = jnp.concatenate([first_row[0:1], last[: wide - 1]], 0)
    after = jnp.concatenate([first_row[1:], last[wide - 1 :]], 0)
    for k, part in enumerate((before, last, after)):
        v_send[:, k] = part.reshape(wide, 1, LANES)

    def post_backward(k, carry):
        to_w = partner(k)
        remote(
            v_send.at[to_w],
            v_recv.at[w],
            phase_send.at[3],
            phase_recv.at[3],
            to_w,
            n,
        ).start()
        return carry

    lax.fori_loop(0, wide - 1, post_backward, 0)
    v_recv[pl.ds(w, 1)] = v_send[pl.ds(w, 1)]
    pltpu.make_async_copy(
        v_recv.at[pl.ds(0, wide - 1)], v_recv.at[pl.ds(0, wide - 1)], phase_recv.at[3]
    ).wait()

    before, last, after = (v_recv[:, k].reshape(wide, LANES) for k in range(3))
    rest_0 = rhs[0] - own_low[0] * before
    rest_1 = rhs[1] - own_high[1] * last
    planes = [
        before,
        block[0] * rest_0 + block[1] * rest_1,
        block[2] * rest_0 + block[3] * rest_1,
        last,
        after,
    ]
    cells = exact_dot(zmat[:, 128 : 128 + wide], jnp.concatenate(planes, 1))
    rims = exact_dot(
        zmat[:, 256 : 256 + CY * wide], jnp.concatenate(planes[1 : CY + 1], 0)
    )
    for k in range(narrow):
        u_send[k, :, 0 : (CY + 2) * LANES] = cells[ZB * k : ZB * (k + 1)]
        u_send[k, :, (CY + 2) * LANES :] = rims[ZB * k : ZB * (k + 1)]
    exchange_narrow(u_send, u_recv, 4)

    locals_[5].wait()
    locals_[6].wait()
    rows = [
        jnp.concatenate(
            [u_recv[k, :, LANES * r : LANES * (r + 1)] for k in range(narrow)], 1
        )
        for r in range(CY + 3)
    ]
    potential = split_dot(jnp.concatenate(rows, 0), ihigh, ilow)
    length_x = potential.shape[1]
    rim = potential[(CY + 2) * ZB :]
    row_id = lax.broadcasted_iota(jnp.int32, (ZB, length_x), 0)

    for y in range(CY):
        here = potential[(y + 1) * ZB : (y + 2) * ZB]
        below = potential[y * ZB : (y + 1) * ZB]
        above = potential[(y + 2) * ZB : (y + 3) * ZB]
        press_ref[y] = here
        left = jnp.where(row_id == 0, rim[2 * y : 2 * y + 1], pltpu.roll(here, 1, 0))
        right = jnp.where(
            row_id == ZB - 1, rim[2 * y + 1 : 2 * y + 2], pltpu.roll(here, ZB - 1, 0)
        )
        grads = [
            pltpu.roll(here, length_x - 1, 1) - pltpu.roll(here, 1, 1),
            above - below,
            right - left,
        ]
        for f in range(3):
            out_ref[f, y] = out_ref[f, y] - 0.5 * grads[f]

    for halo in halos[cut_a:]:
        halo.wait_send()
    part = sums.at[pl.ds(0, 3 * narrow - 1)]
    pltpu.make_async_copy(part, part, phase_send.at[0]).wait()
    for phase, ref in ((1, n_send), (4, u_send)):
        part = ref.at[pl.ds(0, narrow - 1)]
        pltpu.make_async_copy(part, part, phase_send.at[phase]).wait()
    for phase, ref in ((2, w_recv), (3, v_recv)):
        part = ref.at[pl.ds(0, wide - 1)]
        pltpu.make_async_copy(part, part, phase_send.at[phase]).wait()


def body(wide, narrow, consts, fields, y_bands):
    span_here, length_x = fields.shape[2], fields.shape[3]
    tiled = fields.reshape(5, CY, span_here, SUBS, LANES).transpose(0, 1, 3, 2, 4)
    tiled = tiled.reshape(5 * CY * SUBS * span_here, LANES)
    f32 = jnp.float32
    levels = math.ceil(math.log2(wide))
    points = 5 * 5 * (ZB + 2) * SUBS
    vmem = pltpu.VMEM
    scratch = [
        vmem(tiled.shape, f32),
        *[vmem((length_x, length_x), jnp.bfloat16) for _ in range(4)],
        vmem((2 * narrow + 2 * wide, LANES), f32),
        vmem((wide, 512), f32),
        vmem((5, CY + 6, ZB + 6, SUBS, LANES), f32),
        vmem((3, CY + 2, ZB + 4, SUBS, LANES), f32),
        vmem((6, CY, ZB + 2, SUBS, LANES), f32),
        vmem((6, CY, ZB + 2, SUBS, LANES), f32),
        vmem((CY + 2, ZB + 2, SUBS, LANES), f32),
        vmem((3, CY + 2, ZB + 2, SUBS, LANES), f32),
        vmem((points, LANES), f32),
        vmem((points, LANES), f32),
        vmem((points, LANES), f32),
        vmem((CY * ZB * SUBS, LANES), f32),
        vmem((3 * narrow, SUBS, LANES), f32),
        vmem((SUBS, LANES), f32),
        vmem((3, wide * CY, LANES), f32),
        vmem((5, wide, LANES), f32),
        vmem((4, wide, LANES), f32),
        vmem((levels, 2, wide, LANES), f32),
        vmem((narrow, ZB, CY * LANES), f32),
        vmem((narrow, ZB, CY * LANES), f32),
        vmem((wide, 2, 1, LANES), f32),
        vmem((wide, 2, 1, LANES), f32),
        vmem((wide, 3, 1, LANES), f32),
        vmem((wide, 3, 1, LANES), f32),
        vmem((narrow, ZB, (CY + 3) * LANES), f32),
        vmem((narrow, ZB, (CY + 3) * LANES), f32),
        pltpu.SemaphoreType.DMA((7,)),
        pltpu.SemaphoreType.REGULAR((wide.bit_length() - 1,)),
        pltpu.SemaphoreType.DMA((24,)),
        pltpu.SemaphoreType.DMA((24,)),
        pltpu.SemaphoreType.DMA((5,)),
        pltpu.SemaphoreType.DMA((5,)),
    ]
    hbm = pl.BlockSpec(memory_space=pltpu.HBM)
    inside = pl.BlockSpec(memory_space=pltpu.VMEM)
    return pl.pallas_call(
        functools.partial(kernel, wide, narrow),
        out_shape=(
            jax.ShapeDtypeStruct(fields.shape, f32),
            jax.ShapeDtypeStruct(fields.shape[1:], f32),
        ),
        in_specs=[hbm, inside, *[hbm] * 5],
        out_specs=(inside, inside),
        scratch_shapes=scratch,
        compiler_params=pltpu.CompilerParams(
            collective_id=0, has_side_effects=True, vmem_limit_bytes=53 * 1024 * 1024
        ),
    )(tiled, y_bands, *consts)


def solution(mesh):
    wide, narrow = mesh.shape["wide"], mesh.shape["narrow"]

    def run(fields, y_bands):
        consts = tables(fields.shape[3], fields.shape[2], wide, narrow)
        consts = [jnp.asarray(table) for table in consts]
        return jax.shard_map(
            functools.partial(body, wide, narrow, consts),
            mesh=mesh,
            in_specs=(P(None, "wide", "narrow", None), P()),
            out_specs=(P(None, "wide", "narrow", None), P("wide", "narrow", None)),
            check_vma=False,
        )(fields, y_bands)

    return run
```

```python
import functools
import math

import jax
import jax.numpy as jnp
import ml_dtypes
import numpy as np
from jax import lax
from jax.experimental import pallas as pl
from jax.experimental.pallas import tpu as pltpu
from jax.sharding import PartitionSpec as P

EPSILON = 1e-06
STEP = 0.05
GRAVITY = 0.5
MOLECULAR = [0.02, 0.02, 0.02, 0.028, 0.04]
TURBULENT = [1.0, 1.0, 1.0, 1.0 / 0.85, 1.0 / 0.7]
PAIRS = [(0, 0), (1, 1), (2, 2), (0, 1), (0, 2), (1, 2)]
LANES = 128
SUBS = 8
CY = 3
ZB = 8


def basis(count):
    half = count // 2
    modes = np.arange(count)
    wave = np.where(modes <= half, modes, modes - half)
    phase = (wave[:, None] * np.arange(count)[None, :]) % count
    angle = 2.0 * math.pi / count * phase
    table = np.where(modes[:, None] <= half, np.cos(angle), np.sin(angle))
    weight = np.where((modes == 0) | (modes == half), 1.0, 2.0) / count
    lam = 2.0 - 2.0 * np.cos(2.0 * math.pi / count * wave)
    return table, weight, lam


def split_table(table):
    high = table.astype(ml_dtypes.bfloat16)
    low = (table - high.astype(np.float64)).astype(ml_dtypes.bfloat16)
    return high, low


@functools.lru_cache
def tables(length_x, span_all, wide, narrow):
    basis_x, weight_x, lam_x = basis(length_x)
    basis_z, weight_z, lam_z = basis(span_all)
    forward = split_table(basis_x.T)
    inverse = split_table(basis_x)
    rows = np.zeros((2 * narrow + 2 * wide, LANES), np.float32)
    rows[0:narrow] = lam_x.reshape(narrow, LANES)
    rows[narrow : 2 * narrow] = weight_x.reshape(narrow, LANES)
    rows[2 * narrow : 2 * narrow + wide] = lam_z[:, None]
    rows[2 * narrow + wide :] = weight_z[:, None]
    zmat = np.zeros((span_all, 512), np.float32)
    zmat[:, 0:span_all] = basis_z
    zmat[:, 128 : 128 + span_all] = basis_z.T
    for n in range(narrow):
        for y in range(CY):
            for side in range(2):
                z = (ZB * n - 1 if side == 0 else ZB * n + ZB) % span_all
                row = ZB * n + 2 * y + side
                zmat[row, 256 + y * span_all : 256 + (y + 1) * span_all] = basis_z[:, z]
    small = np.zeros((length_x, length_x), np.float32)
    small[0 : rows.shape[0], 0:LANES] = rows
    small[0:span_all, LANES : LANES + 512] = zmat
    return (*forward, *inverse, small)


def shift_x(value, step):
    lane = lax.broadcasted_iota(jnp.int32, value.shape, value.ndim - 1)
    if step > 0:
        moved = pltpu.roll(value, LANES - step, value.ndim - 1)
        carried = pltpu.roll(moved, SUBS - 1, value.ndim - 2)
        return jnp.where(lane >= LANES - step, carried, moved)
    moved = pltpu.roll(value, -step, value.ndim - 1)
    carried = pltpu.roll(moved, 1, value.ndim - 2)
    return jnp.where(lane < -step, carried, moved)


def three(below, centre, above):
    return (below + above) + (centre + centre)


def filter_x(value):
    return three(shift_x(value, -1), value, shift_x(value, 1)) * (1.0 / 64.0)


def strain(at, y, z):
    grads = []
    for i in range(3):
        here = at(i, y, z)
        grads.append(
            (
                shift_x(here, 1) - shift_x(here, -1),
                at(i, y + 1, z) - at(i, y - 1, z),
                at(i, y, z + 1) - at(i, y, z - 1),
            )
        )
    parts = [
        grads[i][i] if i == j else 0.5 * (grads[i][j] + grads[j][i]) for i, j in PAIRS
    ]
    diag = parts[0] * parts[0] + parts[1] * parts[1] + parts[2] * parts[2]
    off = parts[3] * parts[3] + parts[4] * parts[4] + parts[5] * parts[5]
    return parts, jnp.sqrt(0.5 * diag + off)


def shift_rows(value, step, filler):
    pad = jnp.full((abs(step), value.shape[1]), filler, value.dtype)
    if step > 0:
        return jnp.concatenate([pad, value[: value.shape[0] - step]], 0)
    return jnp.concatenate([value[-step:], pad], 0)


def exact_dot(left, right):
    return jnp.dot(
        left, right, precision=lax.Precision.HIGHEST, preferred_element_type=jnp.float32
    )


def split_dot(rows, high_ref, low_ref):
    count = rows.shape[0]
    high = rows.astype(jnp.bfloat16)
    low = (rows - high.astype(jnp.float32)).astype(jnp.bfloat16)
    both = jnp.dot(
        jnp.concatenate([high, low], 0), high_ref[...], preferred_element_type=jnp.float32
    )
    rest = jnp.dot(high, low_ref[...], preferred_element_type=jnp.float32)
    return both[:count] + (both[count:] + rest)


def kernel(
    wide,
    narrow,
    fields_hbm,
    bands_ref,
    fhigh_hbm,
    flow_hbm,
    ihigh_hbm,
    ilow_hbm,
    small_hbm,
    out_ref,
    press_ref,
    nat,
    fhigh,
    flow,
    ihigh,
    ilow,
    rowtab,
    zmat,
    pad,
    yfilt,
    ymod,
    yprod,
    mag,
    filt,
    part_a,
    part_b,
    pred,
    div,
    sums,
    mine,
    bands,
    block,
    chain,
    factors,
    n_send,
    n_recv,
    w_send,
    w_recv,
    v_send,
    v_recv,
    u_send,
    u_recv,
    local_sem,
    round_sem,
    halo_send,
    halo_recv,
    phase_send,
    phase_recv,
):
    w = lax.axis_index("wide")
    n = lax.axis_index("narrow")
    w_down, w_up = lax.rem(w + wide - 1, wide), lax.rem(w + 1, wide)
    n_down, n_up = lax.rem(n + narrow - 1, narrow), lax.rem(n + 1, narrow)

    locals_ = [
        pltpu.make_async_copy(src, dst, local_sem.at[k])
        for k, (src, dst) in enumerate(
            [
                (fields_hbm, nat),
                (small_hbm.at[pl.ds(0, rowtab.shape[0]), pl.ds(0, LANES)], rowtab),
                (small_hbm.at[pl.ds(0, zmat.shape[0]), pl.ds(LANES, 512)], zmat),
                (fhigh_hbm, fhigh),
                (flow_hbm, flow),
                (ihigh_hbm, ihigh),
                (ilow_hbm, ilow),
            ]
        )
    ]
    for copy in locals_:
        copy.start()

    barrier = pltpu.get_barrier_semaphore()

    def greet(to_w, to_n):
        pl.semaphore_signal(
            barrier,
            inc=1,
            device_id={"wide": to_w, "narrow": to_n},
            device_id_type=pl.DeviceIdType.MESH,
        )

    for d in range(1, narrow):
        greet(w, lax.rem(n + d, narrow))
    for to_n in (n_down, n_up):
        greet(w_down, to_n)
        greet(w_up, to_n)
    greet(w_up, n)
    rounds = [1 << r for r in range(wide.bit_length() - 1)]
    for reach in rounds:
        greet(lax.rem(w + wide - reach, wide), n)

    def tell(r):
        pl.semaphore_signal(
            round_sem.at[r],
            inc=1,
            device_id={"wide": lax.rem(w + rounds[r], wide), "narrow": n},
            device_id_type=pl.DeviceIdType.MESH,
        )

    def hear(r):
        pl.semaphore_wait(round_sem.at[r], 1)

    def remote(src, dst, send, recv, to_w, to_n):
        return pltpu.make_async_remote_copy(
            src_ref=src,
            dst_ref=dst,
            send_sem=send,
            recv_sem=recv,
            device_id={"wide": to_w, "narrow": to_n},
            device_id_type=pl.DeviceIdType.MESH,
        )

    locals_[0].wait()

    def to_tiles(f, carry):
        for y in range(CY):
            for z in range(ZB):
                pad[f, y + 3, z + 3] = nat[pl.ds((f * CY + y) * 64 + z, SUBS, stride=ZB), :]
        return carry

    lax.fori_loop(0, 5, to_tiles, 0)
    for f in range(3):
        for y in (1, 7):
            for z in (1, 12):
                pad[f, y, z] = jnp.zeros((SUBS, LANES), jnp.float32)

    pl.semaphore_wait(barrier, (narrow - 1) + 5 + len(rounds))

    def both(fs, ys, zs):
        return pad.at[pl.ds(*fs), pl.ds(*ys), pl.ds(*zs)]

    own_z = (3, ZB)
    own_y = (3, CY)
    vel, sca = (0, 3), (3, 2)
    first = [
        (vel, (3, 2), own_z, (6, 2), own_z, w_down, n),
        (vel, (4, 2), own_z, (1, 2), own_z, w_up, n),
        (vel, (3, 1), (3, 2), (6, 1), (11, 2), w_down, n_down),
        (vel, (3, 1), (9, 2), (6, 1), (1, 2), w_down, n_up),
        (vel, (5, 1), (3, 2), (2, 1), (11, 2), w_up, n_down),
        (vel, (5, 1), (9, 2), (2, 1), (1, 2), w_up, n_up),
        (vel, (4, 1), (3, 1), (7, 1), (11, 1), w_down, n_down),
        (vel, (4, 1), (10, 1), (7, 1), (2, 1), w_down, n_up),
        (vel, (4, 1), (3, 1), (1, 1), (11, 1), w_up, n_down),
        (vel, (4, 1), (10, 1), (1, 1), (2, 1), w_up, n_up),
        (vel, own_y, (3, 2), own_y, (11, 2), w, n_down),
        (vel, own_y, (9, 2), own_y, (1, 2), w, n_up),
    ]
    second = [
        ((1, 1), (5, 1), own_z, (8, 1), own_z, w_down, n),
        ((1, 1), (3, 1), own_z, (0, 1), own_z, w_up, n),
        ((3, 1), (3, 1), own_z, (6, 1), own_z, w_down, n),
        ((3, 1), (5, 1), own_z, (2, 1), own_z, w_up, n),
        ((2, 1), own_y, (5, 1), own_y, (13, 1), w, n_down),
        ((2, 1), own_y, (8, 1), own_y, (0, 1), w, n_up),
    ]
    third = [
        ((3, 1), (4, 1), own_z, (7, 1), own_z, w_down, n),
        ((3, 1), (4, 1), own_z, (1, 1), own_z, w_up, n),
        ((4, 1), (3, 2), own_z, (6, 2), own_z, w_down, n),
        ((4, 1), (4, 2), own_z, (1, 2), own_z, w_up, n),
        (sca, own_y, (3, 2), own_y, (11, 2), w, n_down),
        (sca, own_y, (9, 2), own_y, (1, 2), w, n_up),
    ]
    halos = [
        remote(both(fs, sy, sz), both(fs, ty, tz), halo_send.at[k], halo_recv.at[k], to_w, to_n)
        for k, (fs, sy, sz, ty, tz, to_w, to_n) in enumerate(first + second + third)
    ]
    cut_a, cut_b = len(first), len(first) + len(second)
    for halo in halos[:cut_a]:
        halo.start()
    tell(0)

    locals_[1].wait()
    band = lax.broadcasted_iota(jnp.int32, (3, LANES), 0)
    spread = [
        lax.dot_general(
            bands_ref[...],
            jnp.where(band == k, 1.0, 0.0).astype(jnp.float32),
            (((0,), (0,)), ((), ())),
            precision=lax.Precision.HIGHEST,
            preferred_element_type=jnp.float32,
        )
        for k in range(3)
    ]
    for k in range(3):
        bands[k] = spread[k]

    def invert(low, mid, high):
        det = 1.0 / (mid[0] * mid[1] - high[0] * low[1])
        return mid[1] * det, -high[0] * det, -low[1] * det, mid[0] * det

    lam_x = rowtab[pl.ds(n, 1), :]
    eig = rowtab[2 * narrow : 2 * narrow + wide, :] + lam_x
    own_low, own_mid, own_high = (
        [bands[k, pl.ds(CY * w + j, 1), :] for j in range(CY)] for k in range(3)
    )
    for k, part in enumerate(invert(own_low, [m + eig for m in own_mid[:2]], own_high)):
        block[k] = part
    block[4] = -rowtab[2 * narrow + wide :, :] * rowtab[pl.ds(narrow + n, 1), :]

    eig = lam_x + rowtab[pl.ds(2 * narrow + w, 1), :]
    low, mid, high = (
        [bands[k, pl.ds(j, wide, stride=CY), :] for j in range(CY)] for k in range(3)
    )
    mid = [m + eig for m in mid]
    i00, i01, i10, i11 = invert(low, mid, high)
    from_low, from_high = -i00 * low[0], -i01 * high[1]
    chain[0], chain[1], chain[2] = from_low, from_high, -high[2]
    lower = -low[2] * i10 * low[0]
    diag = mid[2] - low[2] * i11 * high[1] + high[2] * shift_rows(from_low, -1, 0.0)
    upper = high[2] * shift_rows(from_high, -1, 0.0)
    stride = 1
    level = 0
    while stride < wide:
        inv = 1.0 / diag
        to_low = -lower * shift_rows(inv, stride, 1.0)
        to_high = -upper * shift_rows(inv, -stride, 1.0)
        factors[level, 0] = to_low
        factors[level, 1] = to_high
        diag = (
            diag
            + to_low * shift_rows(upper, stride, 0.0)
            + to_high * shift_rows(lower, -stride, 0.0)
        )
        lower = to_low * shift_rows(lower, stride, 0.0)
        upper = to_high * shift_rows(upper, -stride, 0.0)
        stride *= 2
        level += 1
    chain[3] = 1.0 / diag

    hear(0)
    tell(1)
    for halo in halos[:cut_a]:
        halo.wait_send()
    for halo in halos[cut_a:cut_b]:
        halo.start()

    def clear(rows, fields, cells):
        def one(z, carry):
            for f in fields:
                for y in rows:
                    pad[f, y, z] = jnp.zeros((SUBS, LANES), jnp.float32)
            return carry

        lax.fori_loop(cells[0], cells[1], one, 0)

    def outside(below, above, fields, cells):
        @pl.when(w == 0)
        def _():
            for part in cells:
                clear(below, fields, part)

        @pl.when(w == wide - 1)
        def _():
            for part in cells:
                clear(above, fields, part)

    def at_pad(f, y, z):
        return pad[f, y + 3, z + 3]

    def filter_rows(iz, carry):
        z = iz - 2
        for i in range(3):
            column = [at_pad(i, y, z) for y in range(-2, 5)]
            for y in range(5):
                yfilt[i, y, iz] = three(column[y], column[y + 1], column[y + 2])
        return carry


    def local_terms(iz, carry):
        z = iz - 1
        modeled = []
        for y in range(-1, 4):
            parts, size = strain(at_pad, y, z)
            mag[y + 1, iz] = size
            modeled.append([size * part for part in parts])
        for p in range(6):
            for y in range(CY):
                ymod[p, y, iz] = three(modeled[y][p], modeled[y + 1][p], modeled[y + 2][p])
        columns = [[at_pad(i, y, z) for y in range(-1, 4)] for i in range(3)]
        for p, (i, j) in enumerate(PAIRS):
            prods = [columns[i][y] * columns[j][y] for y in range(5)]
            for y in range(CY):
                yprod[p, y, iz] = three(prods[y], prods[y + 1], prods[y + 2])
        for i in range(3):
            for y in range(5):
                value = three(yfilt[i, y, iz], yfilt[i, y, iz + 1], yfilt[i, y, iz + 2])
                filt[i, y, iz] = filter_x(value)
        return carry


    def at_filt(f, y, z):
        return filt[f, y + 1, z + 1]

    def plane_terms(z, carry):
        cross, square = list(carry[0]), list(carry[1])
        for y in range(CY):
            parts, size = strain(at_filt, y, z)
            centre = [at_filt(i, y, z) for i in range(3)]
            four = 4.0 * size
            lm_diag = lm_off = mm_diag = mm_off = None
            for p, (i, j) in enumerate(PAIRS):
                model = filter_x(three(ymod[p, y, z], ymod[p, y, z + 1], ymod[p, y, z + 2]))
                model = model - four * parts[p]
                stress = filter_x(three(yprod[p, y, z], yprod[p, y, z + 1], yprod[p, y, z + 2]))
                stress = stress - centre[i] * centre[j]
                if p < 3:
                    lm_diag = stress * model if lm_diag is None else lm_diag + stress * model
                    mm_diag = model * model if mm_diag is None else mm_diag + model * model
                else:
                    lm_off = stress * model if lm_off is None else lm_off + stress * model
                    mm_off = model * model if mm_off is None else mm_off + model * model
            cross[y] = cross[y] + (lm_diag + (lm_off + lm_off))
            square[y] = square[y] + (mm_diag + (mm_off + mm_off))
        return tuple(cross), tuple(square)

    nothing = jnp.zeros((SUBS, LANES), jnp.float32)
    plane = ((nothing,) * CY, (nothing,) * CY)

    def edges(step, inner):
        return lambda k, carry: step(k + lax.div(k, 2) * inner, carry)

    inner_cells, rim_cells = (3, ZB + 3), ((1, 3), (ZB + 3, ZB + 5))
    for halo in halos[:2]:
        halo.wait_recv()
    hear(1)
    tell(2)
    outside((1, 2), (6, 7), range(3), (inner_cells,))
    lax.fori_loop(2, ZB + 2, filter_rows, 0)
    lax.fori_loop(2, ZB, local_terms, 0)
    plane = lax.fori_loop(2, ZB - 2, plane_terms, plane)
    for halo in halos[2:cut_a]:
        halo.wait_recv()
    outside((1, 2), (6, 7), range(3), rim_cells)
    lax.fori_loop(0, 4, edges(filter_rows, ZB), 0)
    lax.fori_loop(0, 4, edges(local_terms, ZB - 2), 0)
    cross, square = lax.fori_loop(0, 4, edges(plane_terms, ZB - 4), plane)
    packed = [jnp.sum(v, 0, keepdims=True) for v in (*cross, *square)]
    packed.append(jnp.zeros((SUBS - 2 * CY, LANES), jnp.float32))
    tile = jnp.concatenate(packed, 0)
    tile = jnp.broadcast_to(jnp.sum(tile, 1, keepdims=True), (SUBS, LANES))
    mine[...] = tile
    sums[pl.ds(narrow + n, 1)] = tile[None]
    half_n = narrow // 2
    side_n, cell_n = lax.div(n, half_n), lax.rem(n, half_n)
    others = []
    for d_side, d_cell in ((1, 2), (1, 1), (1, 3), (0, 2), (1, 0), (0, 1), (0, 3)):
        others.append(
            lax.rem(side_n + d_side, 2) * half_n + lax.rem(cell_n + d_cell, half_n)
        )
    peers = [(w_down, 2), (w_up, 0), (w, 1)]
    for to_n in (*others, n):
        for to_w, slot in peers:
            if to_n is n and slot == 1:
                continue
            remote(
                mine,
                sums.at[slot * narrow + n],
                phase_send.at[0],
                phase_recv.at[0],
                to_w,
                to_n,
            ).start()

    for halo in halos[cut_b:]:
        halo.start()
    hear(2)
    tell(3)
    for halo in halos[cut_a:cut_b]:
        halo.wait_recv()
    outside((2,), (6,), (3,), (inner_cells,))
    outside((0,), (8,), (1,), (inner_cells,))

    def slot_of(f, y, z):
        return pl.ds(pl.multiple_of(((f * 5 + y + 1) * (ZB + 2) + z + 1) * SUBS, SUBS), SUBS)

    def advance(fs, y, z):
        velocity = [at_pad(i, y, z) for i in range(3)]
        size = mag[y + 1, z + 1]
        for f in fs:
            here = velocity[f] if f < 3 else at_pad(f, y, z)
            xp, xm = shift_x(here, 1), shift_x(here, -1)
            yp, ym = at_pad(f, y + 1, z), at_pad(f, y - 1, z)
            zp, zm = at_pad(f, y, z + 1), at_pad(f, y, z - 1)
            ex = 8.0 * (xp - xm) - (shift_x(here, 2) - shift_x(here, -2))
            ey = 8.0 * (yp - ym) - (at_pad(f, y + 2, z) - at_pad(f, y - 2, z))
            ez = 8.0 * (zp - zm) - (at_pad(f, y, z + 2) - at_pad(f, y, z - 2))
            carried = velocity[0] * ex + velocity[1] * ey + velocity[2] * ez
            lap = ((xp + xm) + (yp + ym)) + ((zp + zm) - 6.0 * here)
            value = here - (STEP / 12.0) * carried + (STEP * MOLECULAR[f]) * lap
            if f == 1:
                value = value + (STEP * GRAVITY) * at_pad(3, y, z)
            part_a[slot_of(f, y, z), :] = value
            part_b[slot_of(f, y, z), :] = (STEP * TURBULENT[f]) * (size * lap)

    def advance_cells(z, carry):
        for y in range(CY):
            advance(range(3), y, z)
        advance((1,), -1, z)
        advance((1,), CY, z)
        return carry

    lax.fori_loop(0, ZB, advance_cells, 0)
    for y in range(CY):
        advance((2,), y, -1)
        advance((2,), y, ZB)

    inside_low = jnp.where(w == 0, 0.0, 1.0)
    inside_high = jnp.where(w == wide - 1, 0.0, 1.0)

    def store(row, value):
        div[pl.ds(pl.multiple_of(row * SUBS, SUBS), SUBS), :] = value

    def divergence(z, carry):
        def get(part, f, y):
            value = part[slot_of(f, y, z), :]
            if y < 0:
                return value * inside_low
            return value * inside_high if y == CY else value

        wall_a = [get(part_a, 1, y) for y in range(-1, CY + 1)]
        for y in range(CY):
            for first_row, part in ((0, part_a), (CY * ZB, part_b)):
                stream = part[slot_of(0, y, z), :]
                value = shift_x(stream, 1) - shift_x(stream, -1)
                value = value + (part[slot_of(2, y, z + 1), :] - part[slot_of(2, y, z - 1), :])
                if first_row == 0:
                    value = value + (wall_a[y + 2] - wall_a[y])
                store(first_row + y * ZB + z, 0.5 * value)
        for y in range(-1, CY + 1):
            store((2 * CY + y + 1) * ZB + z, 0.5 * get(part_b, 1, y))
        return carry

    lax.fori_loop(0, ZB, divergence, 0)
    count = (3 * CY + 2) * ZB
    hear(3)
    tell(4)
    locals_[3].wait()
    locals_[4].wait()
    flat = jnp.concatenate([div[pl.ds(s, count, stride=SUBS), :] for s in range(SUBS)], 1)
    flat = jnp.concatenate([flat, jnp.zeros((8, flat.shape[1]), jnp.float32)], 0)
    spectrum = split_dot(flat, fhigh, flow)

    pltpu.make_async_copy(
        sums.at[pl.ds(0, 3 * narrow - 1)], sums.at[pl.ds(0, 3 * narrow - 1)], phase_recv.at[0]
    ).wait()
    coef = []
    for slot, rows in ((0, (2,)), (1, (0, 1, 2)), (2, (0,))):
        total = sums[slot * narrow]
        for k in range(1, narrow):
            total = total + sums[slot * narrow + k]
        for row in rows:
            ratio = total[row : row + 1] / (total[CY + row : CY + row + 1] + EPSILON)
            coef.append(jnp.broadcast_to(ratio, (SUBS, LANES)))

    for k in range(narrow):
        part = spectrum[:, LANES * k : LANES * (k + 1)]
        tiles = [part[ZB * r : ZB * (r + 1)] for r in range(3 * CY + 2)]
        walls = [coef[r] * tiles[2 * CY + r] for r in range(CY + 2)]
        for y in range(CY):
            n_send[k, :, LANES * y : LANES * (y + 1)] = (
                tiles[y] + coef[y + 1] * tiles[CY + y] + (walls[y + 2] - walls[y])
            )

    def exchange_narrow(source, target, phase):
        for to_n in others:
            remote(
                source.at[to_n], target.at[n], phase_send.at[phase], phase_recv.at[phase], w, to_n
            ).start()
        target[pl.ds(n, 1)] = source[pl.ds(n, 1)]
        pltpu.make_async_copy(
            target.at[pl.ds(0, narrow - 1)],
            target.at[pl.ds(0, narrow - 1)],
            phase_recv.at[phase],
        ).wait()

    hear(4)
    tell(5)
    exchange_narrow(n_send, n_recv, 1)
    locals_[2].wait()
    spanwise = exact_dot(
        zmat[:, 0:wide], n_recv[...].reshape(narrow * ZB, CY * LANES)
    )
    rhs = [spanwise[:, LANES * y : LANES * (y + 1)] * block[4] for y in range(CY)]
    inner_0 = block[0] * rhs[0] + block[1] * rhs[1]
    inner_1 = block[2] * rhs[0] + block[3] * rhs[1]
    w_send[:, 0] = inner_0.reshape(wide, 1, LANES)
    w_send[:, 1] = (rhs[2] - own_low[2] * inner_1).reshape(wide, 1, LANES)

    depth = wide // 8
    w_z, w_y, w_c = lax.div(w, 8), lax.rem(lax.div(w, 2), 4), lax.rem(w, 2)

    def swing(k):
        return lax.div(k, 2) * (1 - 2 * lax.rem(k, 2)) - lax.rem(k, 2)

    def partner(k):
        to_z = lax.rem(w_z + depth // 2 + swing(lax.div(k, 8)) + depth, depth)
        to_y = lax.rem(w_y + 2 + swing(lax.rem(lax.div(k, 2), 4)) + 4, 4)
        to_c = lax.rem(w_c + 1 - lax.rem(k, 2), 2)
        return (to_z * 4 + to_y) * 2 + to_c

    def post_forward(k, carry):
        to_w = partner(k)
        remote(
            w_send.at[to_w], w_recv.at[w], phase_send.at[2], phase_recv.at[2], to_w, n
        ).start()
        return carry

    hear(5)
    lax.fori_loop(0, wide - 1, post_forward, 0)
    w_recv[pl.ds(w, 1)] = w_send[pl.ds(w, 1)]

    for halo in halos[cut_b:]:
        halo.wait_recv()

    outside((1, 2), (6, 7), (3, 4), (inner_cells,))

    def finish(f, y, z):
        pred[slot_of(f, y, z), :] = (
            part_a[slot_of(f, y, z), :] + coef[y + 1] * part_b[slot_of(f, y, z), :]
        )

    def scalar_cells(z, carry):
        for y in range(CY):
            advance((3, 4), y, z)
            for f in range(5):
                finish(f, y, z)
        return carry

    lax.fori_loop(0, ZB, scalar_cells, 0)

    def to_rows(f, carry):
        for y in range(CY):
            for s in range(SUBS):
                start = ((f * 5 + y + 1) * (ZB + 2) + 1) * SUBS + s
                out_ref[f, y, :, LANES * s : LANES * (s + 1)] = pred[
                    pl.ds(start, ZB, stride=SUBS), :
                ]
        return carry

    lax.fori_loop(0, 5, to_rows, 0)
    pltpu.make_async_copy(
        w_recv.at[pl.ds(0, wide - 1)], w_recv.at[pl.ds(0, wide - 1)], phase_recv.at[2]
    ).wait()

    first_row = w_recv[:, 0].reshape(wide, LANES)
    last = w_recv[:, 1].reshape(wide, LANES) + chain[2] * shift_rows(first_row, -1, 0.0)
    stride = 1
    level = 0
    while stride < wide:
        last = (
            last
            + factors[level, 0] * shift_rows(last, stride, 0.0)
            + factors[level, 1] * shift_rows(last, -stride, 0.0)
        )
        stride *= 2
        level += 1
    last = last * chain[3]
    before = shift_rows(last, 1, 0.0)
    first_row = first_row + chain[0] * before + chain[1] * last
    before = jnp.concatenate([first_row[0:1], last[: wide - 1]], 0)
    after = jnp.concatenate([first_row[1:], last[wide - 1 :]], 0)
    for k, part in enumerate((before, last, after)):
        v_send[:, k] = part.reshape(wide, 1, LANES)

    def post_backward(k, carry):
        to_w = partner(k)
        remote(
            v_send.at[to_w],
            v_recv.at[w],
            phase_send.at[3],
            phase_recv.at[3],
            to_w,
            n,
        ).start()
        return carry

    lax.fori_loop(0, wide - 1, post_backward, 0)
    v_recv[pl.ds(w, 1)] = v_send[pl.ds(w, 1)]
    pltpu.make_async_copy(
        v_recv.at[pl.ds(0, wide - 1)], v_recv.at[pl.ds(0, wide - 1)], phase_recv.at[3]
    ).wait()

    before, last, after = (v_recv[:, k].reshape(wide, LANES) for k in range(3))
    rest_0 = rhs[0] - own_low[0] * before
    rest_1 = rhs[1] - own_high[1] * last
    planes = [
        before,
        block[0] * rest_0 + block[1] * rest_1,
        block[2] * rest_0 + block[3] * rest_1,
        last,
        after,
    ]
    cells = exact_dot(zmat[:, 128 : 128 + wide], jnp.concatenate(planes, 1))
    rims = exact_dot(
        zmat[:, 256 : 256 + CY * wide], jnp.concatenate(planes[1 : CY + 1], 0)
    )
    for k in range(narrow):
        u_send[k, :, 0 : (CY + 2) * LANES] = cells[ZB * k : ZB * (k + 1)]
        u_send[k, :, (CY + 2) * LANES :] = rims[ZB * k : ZB * (k + 1)]
    exchange_narrow(u_send, u_recv, 4)

    locals_[5].wait()
    locals_[6].wait()
    rows = [
        jnp.concatenate(
            [u_recv[k, :, LANES * r : LANES * (r + 1)] for k in range(narrow)], 1
        )
        for r in range(CY + 3)
    ]
    potential = split_dot(jnp.concatenate(rows, 0), ihigh, ilow)
    length_x = potential.shape[1]
    rim = potential[(CY + 2) * ZB :]
    row_id = lax.broadcasted_iota(jnp.int32, (ZB, length_x), 0)

    for y in range(CY):
        here = potential[(y + 1) * ZB : (y + 2) * ZB]
        below = potential[y * ZB : (y + 1) * ZB]
        above = potential[(y + 2) * ZB : (y + 3) * ZB]
        press_ref[y] = here
        left = jnp.where(row_id == 0, rim[2 * y : 2 * y + 1], pltpu.roll(here, 1, 0))
        right = jnp.where(
            row_id == ZB - 1, rim[2 * y + 1 : 2 * y + 2], pltpu.roll(here, ZB - 1, 0)
        )
        grads = [
            pltpu.roll(here, length_x - 1, 1) - pltpu.roll(here, 1, 1),
            above - below,
            right - left,
        ]
        for f in range(3):
            out_ref[f, y] = out_ref[f, y] - 0.5 * grads[f]

    for halo in halos[cut_a:]:
        halo.wait_send()
    part = sums.at[pl.ds(0, 3 * narrow - 1)]
    pltpu.make_async_copy(part, part, phase_send.at[0]).wait()
    for phase, ref in ((1, n_send), (4, u_send)):
        part = ref.at[pl.ds(0, narrow - 1)]
        pltpu.make_async_copy(part, part, phase_send.at[phase]).wait()
    for phase, ref in ((2, w_recv), (3, v_recv)):
        part = ref.at[pl.ds(0, wide - 1)]
        pltpu.make_async_copy(part, part, phase_send.at[phase]).wait()


def body(wide, narrow, consts, fields, y_bands):
    span_here, length_x = fields.shape[2], fields.shape[3]
    tiled = fields.reshape(5, CY, span_here, SUBS, LANES).transpose(0, 1, 3, 2, 4)
    tiled = tiled.reshape(5 * CY * SUBS * span_here, LANES)
    f32 = jnp.float32
    levels = math.ceil(math.log2(wide))
    points = 5 * 5 * (ZB + 2) * SUBS
    vmem = pltpu.VMEM
    scratch = [
        vmem(tiled.shape, f32),
        *[vmem((length_x, length_x), jnp.bfloat16) for _ in range(4)],
        vmem((2 * narrow + 2 * wide, LANES), f32),
        vmem((wide, 512), f32),
        vmem((5, CY + 6, ZB + 6, SUBS, LANES), f32),
        vmem((3, CY + 2, ZB + 4, SUBS, LANES), f32),
        vmem((6, CY, ZB + 2, SUBS, LANES), f32),
        vmem((6, CY, ZB + 2, SUBS, LANES), f32),
        vmem((CY + 2, ZB + 2, SUBS, LANES), f32),
        vmem((3, CY + 2, ZB + 2, SUBS, LANES), f32),
        vmem((points, LANES), f32),
        vmem((points, LANES), f32),
        vmem((points, LANES), f32),
        vmem(((3 * CY + 2) * ZB * SUBS, LANES), f32),
        vmem((3 * narrow, SUBS, LANES), f32),
        vmem((SUBS, LANES), f32),
        vmem((3, wide * CY, LANES), f32),
        vmem((5, wide, LANES), f32),
        vmem((4, wide, LANES), f32),
        vmem((levels, 2, wide, LANES), f32),
        vmem((narrow, ZB, CY * LANES), f32),
        vmem((narrow, ZB, CY * LANES), f32),
        vmem((wide, 2, 1, LANES), f32),
        vmem((wide, 2, 1, LANES), f32),
        vmem((wide, 3, 1, LANES), f32),
        vmem((wide, 3, 1, LANES), f32),
        vmem((narrow, ZB, (CY + 3) * LANES), f32),
        vmem((narrow, ZB, (CY + 3) * LANES), f32),
        pltpu.SemaphoreType.DMA((7,)),
        pltpu.SemaphoreType.REGULAR((wide.bit_length() - 1,)),
        pltpu.SemaphoreType.DMA((24,)),
        pltpu.SemaphoreType.DMA((24,)),
        pltpu.SemaphoreType.DMA((5,)),
        pltpu.SemaphoreType.DMA((5,)),
    ]
    hbm = pl.BlockSpec(memory_space=pltpu.HBM)
    inside = pl.BlockSpec(memory_space=pltpu.VMEM)
    return pl.pallas_call(
        functools.partial(kernel, wide, narrow),
        out_shape=(
            jax.ShapeDtypeStruct(fields.shape, f32),
            jax.ShapeDtypeStruct(fields.shape[1:], f32),
        ),
        in_specs=[hbm, inside, *[hbm] * 5],
        out_specs=(inside, inside),
        scratch_shapes=scratch,
        compiler_params=pltpu.CompilerParams(
            collective_id=0, has_side_effects=True, vmem_limit_bytes=53 * 1024 * 1024
        ),
    )(tiled, y_bands, *consts)


def solution(mesh):
    wide, narrow = mesh.shape["wide"], mesh.shape["narrow"]

    def run(fields, y_bands):
        consts = tables(fields.shape[3], fields.shape[2], wide, narrow)
        consts = [jnp.asarray(table) for table in consts]
        return jax.shard_map(
            functools.partial(body, wide, narrow, consts),
            mesh=mesh,
            in_specs=(P(None, "wide", "narrow", None), P()),
            out_specs=(P(None, "wide", "narrow", None), P("wide", "narrow", None)),
            check_vma=False,
        )(fields, y_bands)

    return run
```

```python
import functools
import math

import jax
import jax.numpy as jnp
import ml_dtypes
import numpy as np
from jax import lax
from jax.experimental import pallas as pl
from jax.experimental.pallas import tpu as pltpu
from jax.sharding import PartitionSpec as P

EPSILON = 1e-06
STEP = 0.05
GRAVITY = 0.5
MOLECULAR = [0.02, 0.02, 0.02, 0.028, 0.04]
TURBULENT = [1.0, 1.0, 1.0, 1.0 / 0.85, 1.0 / 0.7]
PAIRS = [(0, 0), (1, 1), (2, 2), (0, 1), (0, 2), (1, 2)]
LANES = 128
SUBS = 8
CY = 3
ZB = 8


def basis(count):
    half = count // 2
    modes = np.arange(count)
    wave = np.where(modes <= half, modes, modes - half)
    phase = (wave[:, None] * np.arange(count)[None, :]) % count
    angle = 2.0 * math.pi / count * phase
    table = np.where(modes[:, None] <= half, np.cos(angle), np.sin(angle))
    weight = np.where((modes == 0) | (modes == half), 1.0, 2.0) / count
    lam = 2.0 - 2.0 * np.cos(2.0 * math.pi / count * wave)
    return table, weight, lam


def split_table(table):
    high = table.astype(ml_dtypes.bfloat16)
    low = (table - high.astype(np.float64)).astype(ml_dtypes.bfloat16)
    return high, low


@functools.lru_cache
def tables(length_x, span_all, wide, narrow):
    basis_x, weight_x, lam_x = basis(length_x)
    basis_z, weight_z, lam_z = basis(span_all)
    forward = split_table(basis_x.T)
    inverse = split_table(basis_x)
    rows = np.zeros((2 * narrow + 2 * wide, LANES), np.float32)
    rows[0:narrow] = lam_x.reshape(narrow, LANES)
    rows[narrow : 2 * narrow] = weight_x.reshape(narrow, LANES)
    rows[2 * narrow : 2 * narrow + wide] = lam_z[:, None]
    rows[2 * narrow + wide :] = weight_z[:, None]
    zmat = np.zeros((span_all, 512), np.float32)
    zmat[:, 0:span_all] = basis_z
    zmat[:, 128 : 128 + span_all] = basis_z.T
    for n in range(narrow):
        for y in range(CY):
            for side in range(2):
                z = (ZB * n - 1 if side == 0 else ZB * n + ZB) % span_all
                row = ZB * n + 2 * y + side
                zmat[row, 256 + y * span_all : 256 + (y + 1) * span_all] = basis_z[:, z]
    small = np.zeros((length_x, length_x), np.float32)
    small[0 : rows.shape[0], 0:LANES] = rows
    small[0:span_all, LANES : LANES + 512] = zmat
    return (*forward, *inverse, small)


def shift_x(value, step):
    lane = lax.broadcasted_iota(jnp.int32, value.shape, value.ndim - 1)
    if step > 0:
        moved = pltpu.roll(value, LANES - step, value.ndim - 1)
        carried = pltpu.roll(moved, SUBS - 1, value.ndim - 2)
        return jnp.where(lane >= LANES - step, carried, moved)
    moved = pltpu.roll(value, -step, value.ndim - 1)
    carried = pltpu.roll(moved, 1, value.ndim - 2)
    return jnp.where(lane < -step, carried, moved)


def three(below, centre, above):
    return (below + above) + (centre + centre)


def filter_x(value):
    return three(shift_x(value, -1), value, shift_x(value, 1)) * (1.0 / 64.0)


def strain(at, y, z):
    grads = []
    for i in range(3):
        here = at(i, y, z)
        grads.append(
            (
                shift_x(here, 1) - shift_x(here, -1),
                at(i, y + 1, z) - at(i, y - 1, z),
                at(i, y, z + 1) - at(i, y, z - 1),
            )
        )
    parts = [
        grads[i][i] if i == j else 0.5 * (grads[i][j] + grads[j][i]) for i, j in PAIRS
    ]
    diag = parts[0] * parts[0] + parts[1] * parts[1] + parts[2] * parts[2]
    off = parts[3] * parts[3] + parts[4] * parts[4] + parts[5] * parts[5]
    return parts, jnp.sqrt(0.5 * diag + off)


def shift_rows(value, step, filler):
    pad = jnp.full((abs(step), value.shape[1]), filler, value.dtype)
    if step > 0:
        return jnp.concatenate([pad, value[: value.shape[0] - step]], 0)
    return jnp.concatenate([value[-step:], pad], 0)


def halves(value):
    high = value.astype(jnp.bfloat16)
    return high, (value - high.astype(jnp.float32)).astype(jnp.bfloat16)


def exact_dot(left, right):
    count = left.shape[0]
    left_high, left_low = halves(left)
    right_high, right_low = halves(right)
    both = jnp.dot(
        jnp.concatenate([left_high, left_low], 0),
        right_high,
        preferred_element_type=jnp.float32,
    )
    rest = jnp.dot(left_high, right_low, preferred_element_type=jnp.float32)
    return both[:count] + (both[count:] + rest)


def split_dot(rows, high_ref, low_ref):
    count = rows.shape[0]
    high = rows.astype(jnp.bfloat16)
    low = (rows - high.astype(jnp.float32)).astype(jnp.bfloat16)
    both = jnp.dot(
        jnp.concatenate([high, low], 0), high_ref[...], preferred_element_type=jnp.float32
    )
    rest = jnp.dot(high, low_ref[...], preferred_element_type=jnp.float32)
    return both[:count] + (both[count:] + rest)


def kernel(
    wide,
    narrow,
    fields_hbm,
    bands_ref,
    fhigh_hbm,
    flow_hbm,
    ihigh_hbm,
    ilow_hbm,
    small_hbm,
    out_ref,
    press_ref,
    nat,
    fhigh,
    flow,
    ihigh,
    ilow,
    rowtab,
    zmat,
    pad,
    yfilt,
    ymod,
    yprod,
    mag,
    filt,
    part_a,
    part_b,
    pred,
    div,
    sums,
    mine,
    bands,
    block,
    chain,
    factors,
    n_send,
    n_recv,
    w_send,
    w_recv,
    v_send,
    v_recv,
    u_send,
    u_recv,
    local_sem,
    round_sem,
    halo_send,
    halo_recv,
    phase_send,
    phase_recv,
):
    w = lax.axis_index("wide")
    n = lax.axis_index("narrow")
    w_down, w_up = lax.rem(w + wide - 1, wide), lax.rem(w + 1, wide)
    n_down, n_up = lax.rem(n + narrow - 1, narrow), lax.rem(n + 1, narrow)

    locals_ = [
        pltpu.make_async_copy(src, dst, local_sem.at[k])
        for k, (src, dst) in enumerate(
            [
                (fields_hbm, nat),
                (small_hbm.at[pl.ds(0, rowtab.shape[0]), pl.ds(0, LANES)], rowtab),
                (small_hbm.at[pl.ds(0, zmat.shape[0]), pl.ds(LANES, 512)], zmat),
                (fhigh_hbm, fhigh),
                (flow_hbm, flow),
                (ihigh_hbm, ihigh),
                (ilow_hbm, ilow),
            ]
        )
    ]
    locals_[0].start()

    barrier = pltpu.get_barrier_semaphore()

    def greet(to_w, to_n):
        pl.semaphore_signal(
            barrier,
            inc=1,
            device_id={"wide": to_w, "narrow": to_n},
            device_id_type=pl.DeviceIdType.MESH,
        )

    for d in range(1, narrow):
        greet(w, lax.rem(n + d, narrow))
    for to_n in (n_down, n_up):
        greet(w_down, to_n)
        greet(w_up, to_n)
    greet(w_up, n)
    rounds = [1 << r for r in range(wide.bit_length() - 1)]
    for reach in rounds:
        greet(lax.rem(w + wide - reach, wide), n)

    def tell(r):
        pl.semaphore_signal(
            round_sem.at[r],
            inc=1,
            device_id={"wide": lax.rem(w + rounds[r], wide), "narrow": n},
            device_id_type=pl.DeviceIdType.MESH,
        )

    def hear(r):
        pl.semaphore_wait(round_sem.at[r], 1)

    def remote(src, dst, send, recv, to_w, to_n):
        return pltpu.make_async_remote_copy(
            src_ref=src,
            dst_ref=dst,
            send_sem=send,
            recv_sem=recv,
            device_id={"wide": to_w, "narrow": to_n},
            device_id_type=pl.DeviceIdType.MESH,
        )

    locals_[0].wait()

    def to_tiles(f, carry):
        for y in range(CY):
            for z in range(ZB):
                pad[f, y + 3, z + 3] = nat[pl.ds((f * CY + y) * 64 + z, SUBS, stride=ZB), :]
        return carry

    lax.fori_loop(0, 5, to_tiles, 0)
    for f in range(3):
        for y in (1, 7):
            for z in (1, 12):
                pad[f, y, z] = jnp.zeros((SUBS, LANES), jnp.float32)

    pl.semaphore_wait(barrier, (narrow - 1) + 5 + len(rounds))

    def both(fs, ys, zs):
        return pad.at[pl.ds(*fs), pl.ds(*ys), pl.ds(*zs)]

    own_z = (3, ZB)
    own_y = (3, CY)
    vel, sca = (0, 3), (3, 2)
    first = [
        (vel, (3, 2), own_z, (6, 2), own_z, w_down, n),
        (vel, (4, 2), own_z, (1, 2), own_z, w_up, n),
        (vel, (3, 1), (3, 2), (6, 1), (11, 2), w_down, n_down),
        (vel, (3, 1), (9, 2), (6, 1), (1, 2), w_down, n_up),
        (vel, (5, 1), (3, 2), (2, 1), (11, 2), w_up, n_down),
        (vel, (5, 1), (9, 2), (2, 1), (1, 2), w_up, n_up),
        (vel, (4, 1), (3, 1), (7, 1), (11, 1), w_down, n_down),
        (vel, (4, 1), (10, 1), (7, 1), (2, 1), w_down, n_up),
        (vel, (4, 1), (3, 1), (1, 1), (11, 1), w_up, n_down),
        (vel, (4, 1), (10, 1), (1, 1), (2, 1), w_up, n_up),
        (vel, own_y, (3, 2), own_y, (11, 2), w, n_down),
        (vel, own_y, (9, 2), own_y, (1, 2), w, n_up),
    ]
    second = [
        ((1, 1), (5, 1), own_z, (8, 1), own_z, w_down, n),
        ((1, 1), (3, 1), own_z, (0, 1), own_z, w_up, n),
        ((3, 1), (3, 1), own_z, (6, 1), own_z, w_down, n),
        ((3, 1), (5, 1), own_z, (2, 1), own_z, w_up, n),
        ((2, 1), own_y, (5, 1), own_y, (13, 1), w, n_down),
        ((2, 1), own_y, (8, 1), own_y, (0, 1), w, n_up),
    ]
    third = [
        ((3, 1), (4, 1), own_z, (7, 1), own_z, w_down, n),
        ((3, 1), (4, 1), own_z, (1, 1), own_z, w_up, n),
        ((4, 1), (3, 2), own_z, (6, 2), own_z, w_down, n),
        ((4, 1), (4, 2), own_z, (1, 2), own_z, w_up, n),
        (sca, own_y, (3, 2), own_y, (11, 2), w, n_down),
        (sca, own_y, (9, 2), own_y, (1, 2), w, n_up),
    ]
    halos = [
        remote(both(fs, sy, sz), both(fs, ty, tz), halo_send.at[k], halo_recv.at[k], to_w, to_n)
        for k, (fs, sy, sz, ty, tz, to_w, to_n) in enumerate(first + second + third)
    ]
    cut_a, cut_b = len(first), len(first) + len(second)
    for halo in halos[:cut_a]:
        halo.start()
    tell(0)
    for copy in locals_[1:]:
        copy.start()

    locals_[1].wait()
    band = lax.broadcasted_iota(jnp.int32, (3, LANES), 0)
    spread = [
        lax.dot_general(
            bands_ref[...],
            jnp.where(band == k, 1.0, 0.0).astype(jnp.float32),
            (((0,), (0,)), ((), ())),
            precision=lax.Precision.HIGHEST,
            preferred_element_type=jnp.float32,
        )
        for k in range(3)
    ]
    for k in range(3):
        bands[k] = spread[k]

    def invert(low, mid, high):
        det = 1.0 / (mid[0] * mid[1] - high[0] * low[1])
        return mid[1] * det, -high[0] * det, -low[1] * det, mid[0] * det

    lam_x = rowtab[pl.ds(n, 1), :]
    eig = rowtab[2 * narrow : 2 * narrow + wide, :] + lam_x
    own_low, own_mid, own_high = (
        [bands[k, pl.ds(CY * w + j, 1), :] for j in range(CY)] for k in range(3)
    )
    for k, part in enumerate(invert(own_low, [m + eig for m in own_mid[:2]], own_high)):
        block[k] = part
    block[4] = -rowtab[2 * narrow + wide :, :] * rowtab[pl.ds(narrow + n, 1), :]

    eig = lam_x + rowtab[pl.ds(2 * narrow + w, 1), :]
    low, mid, high = (
        [bands[k, pl.ds(j, wide, stride=CY), :] for j in range(CY)] for k in range(3)
    )
    mid = [m + eig for m in mid]
    i00, i01, i10, i11 = invert(low, mid, high)
    from_low, from_high = -i00 * low[0], -i01 * high[1]
    chain[0], chain[1], chain[2] = from_low, from_high, -high[2]
    lower = -low[2] * i10 * low[0]
    diag = mid[2] - low[2] * i11 * high[1] + high[2] * shift_rows(from_low, -1, 0.0)
    upper = high[2] * shift_rows(from_high, -1, 0.0)
    stride = 1
    level = 0
    while stride < wide:
        inv = 1.0 / diag
        to_low = -lower * shift_rows(inv, stride, 1.0)
        to_high = -upper * shift_rows(inv, -stride, 1.0)
        factors[level, 0] = to_low
        factors[level, 1] = to_high
        diag = (
            diag
            + to_low * shift_rows(upper, stride, 0.0)
            + to_high * shift_rows(lower, -stride, 0.0)
        )
        lower = to_low * shift_rows(lower, stride, 0.0)
        upper = to_high * shift_rows(upper, -stride, 0.0)
        stride *= 2
        level += 1
    chain[3] = 1.0 / diag

    hear(0)
    tell(1)
    for halo in halos[:cut_a]:
        halo.wait_send()
    for halo in halos[cut_a:cut_b]:
        halo.start()

    def clear(rows, fields, cells):
        def one(z, carry):
            for f in fields:
                for y in rows:
                    pad[f, y, z] = jnp.zeros((SUBS, LANES), jnp.float32)
            return carry

        lax.fori_loop(cells[0], cells[1], one, 0)

    def outside(below, above, fields, cells):
        @pl.when(w == 0)
        def _():
            for part in cells:
                clear(below, fields, part)

        @pl.when(w == wide - 1)
        def _():
            for part in cells:
                clear(above, fields, part)

    def at_pad(f, y, z):
        return pad[f, y + 3, z + 3]

    def filter_rows(iz, carry):
        z = iz - 2
        for i in range(3):
            column = [at_pad(i, y, z) for y in range(-2, 5)]
            for y in range(5):
                yfilt[i, y, iz] = three(column[y], column[y + 1], column[y + 2])
        return carry


    def local_terms(iz, carry):
        z = iz - 1
        modeled = []
        for y in range(-1, 4):
            parts, size = strain(at_pad, y, z)
            mag[y + 1, iz] = size
            modeled.append([size * part for part in parts])
        for p in range(6):
            for y in range(CY):
                ymod[p, y, iz] = three(modeled[y][p], modeled[y + 1][p], modeled[y + 2][p])
        columns = [[at_pad(i, y, z) for y in range(-1, 4)] for i in range(3)]
        for p, (i, j) in enumerate(PAIRS):
            prods = [columns[i][y] * columns[j][y] for y in range(5)]
            for y in range(CY):
                yprod[p, y, iz] = three(prods[y], prods[y + 1], prods[y + 2])
        for i in range(3):
            for y in range(5):
                value = three(yfilt[i, y, iz], yfilt[i, y, iz + 1], yfilt[i, y, iz + 2])
                filt[i, y, iz] = filter_x(value)
        return carry


    def at_filt(f, y, z):
        return filt[f, y + 1, z + 1]

    def plane_terms(z, carry):
        cross, square = list(carry[0]), list(carry[1])
        for y in range(CY):
            parts, size = strain(at_filt, y, z)
            centre = [at_filt(i, y, z) for i in range(3)]
            four = 4.0 * size
            lm_diag = lm_off = mm_diag = mm_off = None
            for p, (i, j) in enumerate(PAIRS):
                model = filter_x(three(ymod[p, y, z], ymod[p, y, z + 1], ymod[p, y, z + 2]))
                model = model - four * parts[p]
                stress = filter_x(three(yprod[p, y, z], yprod[p, y, z + 1], yprod[p, y, z + 2]))
                stress = stress - centre[i] * centre[j]
                if p < 3:
                    lm_diag = stress * model if lm_diag is None else lm_diag + stress * model
                    mm_diag = model * model if mm_diag is None else mm_diag + model * model
                else:
                    lm_off = stress * model if lm_off is None else lm_off + stress * model
                    mm_off = model * model if mm_off is None else mm_off + model * model
            cross[y] = cross[y] + (lm_diag + (lm_off + lm_off))
            square[y] = square[y] + (mm_diag + (mm_off + mm_off))
        return tuple(cross), tuple(square)

    nothing = jnp.zeros((SUBS, LANES), jnp.float32)
    plane = ((nothing,) * CY, (nothing,) * CY)

    def edges(step, inner):
        return lambda k, carry: step(k + lax.div(k, 2) * inner, carry)

    inner_cells, rim_cells = (3, ZB + 3), ((1, 3), (ZB + 3, ZB + 5))
    for halo in halos[:2]:
        halo.wait_recv()
    hear(1)
    tell(2)
    outside((1, 2), (6, 7), range(3), (inner_cells,))
    lax.fori_loop(2, ZB + 2, filter_rows, 0)
    lax.fori_loop(2, ZB, local_terms, 0)
    plane = lax.fori_loop(2, ZB - 2, plane_terms, plane)
    for halo in halos[2:cut_a]:
        halo.wait_recv()
    outside((1, 2), (6, 7), range(3), rim_cells)
    lax.fori_loop(0, 4, edges(filter_rows, ZB), 0)
    lax.fori_loop(0, 4, edges(local_terms, ZB - 2), 0)
    cross, square = lax.fori_loop(0, 4, edges(plane_terms, ZB - 4), plane)
    packed = [jnp.sum(v, 0, keepdims=True) for v in (*cross, *square)]
    packed.append(jnp.zeros((SUBS - 2 * CY, LANES), jnp.float32))
    tile = jnp.concatenate(packed, 0)
    tile = jnp.broadcast_to(jnp.sum(tile, 1, keepdims=True), (SUBS, LANES))
    mine[...] = tile
    sums[pl.ds(narrow + n, 1)] = tile[None]
    half_n = narrow // 2
    side_n, cell_n = lax.div(n, half_n), lax.rem(n, half_n)
    others = []
    for d_side, d_cell in ((1, 2), (1, 1), (1, 3), (0, 2), (1, 0), (0, 1), (0, 3)):
        others.append(
            lax.rem(side_n + d_side, 2) * half_n + lax.rem(cell_n + d_cell, half_n)
        )
    peers = [(w_down, 2), (w_up, 0), (w, 1)]
    for to_n in (*others, n):
        for to_w, slot in peers:
            if to_n is n and slot == 1:
                continue
            remote(
                mine,
                sums.at[slot * narrow + n],
                phase_send.at[0],
                phase_recv.at[0],
                to_w,
                to_n,
            ).start()

    for halo in halos[cut_b:]:
        halo.start()
    hear(2)
    tell(3)
    for halo in halos[cut_a:cut_b]:
        halo.wait_recv()
    outside((2,), (6,), (3,), (inner_cells,))
    outside((0,), (8,), (1,), (inner_cells,))

    def slot_of(f, y, z):
        return pl.ds(pl.multiple_of(((f * 5 + y + 1) * (ZB + 2) + z + 1) * SUBS, SUBS), SUBS)

    def advance(fs, y, z):
        velocity = [at_pad(i, y, z) for i in range(3)]
        size = mag[y + 1, z + 1]
        for f in fs:
            here = velocity[f] if f < 3 else at_pad(f, y, z)
            xp, xm = shift_x(here, 1), shift_x(here, -1)
            yp, ym = at_pad(f, y + 1, z), at_pad(f, y - 1, z)
            zp, zm = at_pad(f, y, z + 1), at_pad(f, y, z - 1)
            ex = 8.0 * (xp - xm) - (shift_x(here, 2) - shift_x(here, -2))
            ey = 8.0 * (yp - ym) - (at_pad(f, y + 2, z) - at_pad(f, y - 2, z))
            ez = 8.0 * (zp - zm) - (at_pad(f, y, z + 2) - at_pad(f, y, z - 2))
            carried = velocity[0] * ex + velocity[1] * ey + velocity[2] * ez
            lap = ((xp + xm) + (yp + ym)) + ((zp + zm) - 6.0 * here)
            value = here - (STEP / 12.0) * carried + (STEP * MOLECULAR[f]) * lap
            if f == 1:
                value = value + (STEP * GRAVITY) * at_pad(3, y, z)
            part_a[slot_of(f, y, z), :] = value
            part_b[slot_of(f, y, z), :] = (STEP * TURBULENT[f]) * (size * lap)

    def advance_cells(z, carry):
        for y in range(CY):
            advance(range(3), y, z)
        advance((1,), -1, z)
        advance((1,), CY, z)
        return carry

    lax.fori_loop(0, ZB, advance_cells, 0)
    for y in range(CY):
        advance((2,), y, -1)
        advance((2,), y, ZB)

    inside_low = jnp.where(w == 0, 0.0, 1.0)
    inside_high = jnp.where(w == wide - 1, 0.0, 1.0)

    def store(row, value):
        div[pl.ds(pl.multiple_of(row * SUBS, SUBS), SUBS), :] = value

    def divergence(z, carry):
        def get(part, f, y):
            value = part[slot_of(f, y, z), :]
            if y < 0:
                return value * inside_low
            return value * inside_high if y == CY else value

        wall_a = [get(part_a, 1, y) for y in range(-1, CY + 1)]
        for y in range(CY):
            for first_row, part in ((0, part_a), (CY * ZB, part_b)):
                stream = part[slot_of(0, y, z), :]
                value = shift_x(stream, 1) - shift_x(stream, -1)
                value = value + (part[slot_of(2, y, z + 1), :] - part[slot_of(2, y, z - 1), :])
                if first_row == 0:
                    value = value + (wall_a[y + 2] - wall_a[y])
                store(first_row + y * ZB + z, 0.5 * value)
        for y in range(-1, CY + 1):
            store((2 * CY + y + 1) * ZB + z, 0.5 * get(part_b, 1, y))
        return carry

    lax.fori_loop(0, ZB, divergence, 0)
    count = (3 * CY + 2) * ZB
    hear(3)
    tell(4)
    locals_[3].wait()
    locals_[4].wait()
    flat = jnp.concatenate([div[pl.ds(s, count, stride=SUBS), :] for s in range(SUBS)], 1)
    flat = jnp.concatenate([flat, jnp.zeros((8, flat.shape[1]), jnp.float32)], 0)
    spectrum = split_dot(flat, fhigh, flow)

    pltpu.make_async_copy(
        sums.at[pl.ds(0, 3 * narrow - 1)], sums.at[pl.ds(0, 3 * narrow - 1)], phase_recv.at[0]
    ).wait()
    coef = []
    for slot, rows in ((0, (2,)), (1, (0, 1, 2)), (2, (0,))):
        total = sums[slot * narrow]
        for k in range(1, narrow):
            total = total + sums[slot * narrow + k]
        for row in rows:
            ratio = total[row : row + 1] / (total[CY + row : CY + row + 1] + EPSILON)
            coef.append(jnp.broadcast_to(ratio, (SUBS, LANES)))

    for k in range(narrow):
        part = spectrum[:, LANES * k : LANES * (k + 1)]
        tiles = [part[ZB * r : ZB * (r + 1)] for r in range(3 * CY + 2)]
        walls = [coef[r] * tiles[2 * CY + r] for r in range(CY + 2)]
        for y in range(CY):
            n_send[k, :, LANES * y : LANES * (y + 1)] = (
                tiles[y] + coef[y + 1] * tiles[CY + y] + (walls[y + 2] - walls[y])
            )

    def exchange_narrow(source, target, phase):
        for to_n in others:
            remote(
                source.at[to_n], target.at[n], phase_send.at[phase], phase_recv.at[phase], w, to_n
            ).start()
        target[pl.ds(n, 1)] = source[pl.ds(n, 1)]
        pltpu.make_async_copy(
            target.at[pl.ds(0, narrow - 1)],
            target.at[pl.ds(0, narrow - 1)],
            phase_recv.at[phase],
        ).wait()

    hear(4)
    tell(5)
    exchange_narrow(n_send, n_recv, 1)
    locals_[2].wait()
    spanwise = exact_dot(
        zmat[:, 0:wide], n_recv[...].reshape(narrow * ZB, CY * LANES)
    )
    rhs = [spanwise[:, LANES * y : LANES * (y + 1)] * block[4] for y in range(CY)]
    inner_0 = block[0] * rhs[0] + block[1] * rhs[1]
    inner_1 = block[2] * rhs[0] + block[3] * rhs[1]
    w_send[:, 0] = inner_0.reshape(wide, 1, LANES)
    w_send[:, 1] = (rhs[2] - own_low[2] * inner_1).reshape(wide, 1, LANES)

    depth = wide // 8
    w_z, w_y, w_c = lax.div(w, 8), lax.rem(lax.div(w, 2), 4), lax.rem(w, 2)

    def swing(k):
        return lax.div(k, 2) * (1 - 2 * lax.rem(k, 2)) - lax.rem(k, 2)

    def partner(k):
        to_z = lax.rem(w_z + depth // 2 + swing(lax.div(k, 8)) + depth, depth)
        to_y = lax.rem(w_y + 2 + swing(lax.rem(lax.div(k, 2), 4)) + 4, 4)
        to_c = lax.rem(w_c + 1 - lax.rem(k, 2), 2)
        return (to_z * 4 + to_y) * 2 + to_c

    def post_forward(k, carry):
        to_w = partner(k)
        remote(
            w_send.at[to_w], w_recv.at[w], phase_send.at[2], phase_recv.at[2], to_w, n
        ).start()
        return carry

    hear(5)
    lax.fori_loop(0, wide - 1, post_forward, 0)
    w_recv[pl.ds(w, 1)] = w_send[pl.ds(w, 1)]

    for halo in halos[cut_b:]:
        halo.wait_recv()

    outside((1, 2), (6, 7), (3, 4), (inner_cells,))

    def finish(f, y, z):
        pred[slot_of(f, y, z), :] = (
            part_a[slot_of(f, y, z), :] + coef[y + 1] * part_b[slot_of(f, y, z), :]
        )

    def scalar_cells(z, carry):
        for y in range(CY):
            advance((3, 4), y, z)
            for f in range(5):
                finish(f, y, z)
        return carry

    lax.fori_loop(0, ZB, scalar_cells, 0)

    def to_rows(f, carry):
        for y in range(CY):
            for s in range(SUBS):
                start = ((f * 5 + y + 1) * (ZB + 2) + 1) * SUBS + s
                out_ref[f, y, :, LANES * s : LANES * (s + 1)] = pred[
                    pl.ds(start, ZB, stride=SUBS), :
                ]
        return carry

    lax.fori_loop(0, 5, to_rows, 0)
    pltpu.make_async_copy(
        w_recv.at[pl.ds(0, wide - 1)], w_recv.at[pl.ds(0, wide - 1)], phase_recv.at[2]
    ).wait()

    first_row = w_recv[:, 0].reshape(wide, LANES)
    last = w_recv[:, 1].reshape(wide, LANES) + chain[2] * shift_rows(first_row, -1, 0.0)
    stride = 1
    level = 0
    while stride < wide:
        last = (
            last
            + factors[level, 0] * shift_rows(last, stride, 0.0)
            + factors[level, 1] * shift_rows(last, -stride, 0.0)
        )
        stride *= 2
        level += 1
    last = last * chain[3]
    before = shift_rows(last, 1, 0.0)
    first_row = first_row + chain[0] * before + chain[1] * last
    before = jnp.concatenate([first_row[0:1], last[: wide - 1]], 0)
    after = jnp.concatenate([first_row[1:], last[wide - 1 :]], 0)
    for k, part in enumerate((before, last, after)):
        v_send[:, k] = part.reshape(wide, 1, LANES)

    def post_backward(k, carry):
        to_w = partner(k)
        remote(
            v_send.at[to_w],
            v_recv.at[w],
            phase_send.at[3],
            phase_recv.at[3],
            to_w,
            n,
        ).start()
        return carry

    lax.fori_loop(0, wide - 1, post_backward, 0)
    v_recv[pl.ds(w, 1)] = v_send[pl.ds(w, 1)]
    pltpu.make_async_copy(
        v_recv.at[pl.ds(0, wide - 1)], v_recv.at[pl.ds(0, wide - 1)], phase_recv.at[3]
    ).wait()

    before, last, after = (v_recv[:, k].reshape(wide, LANES) for k in range(3))
    rest_0 = rhs[0] - own_low[0] * before
    rest_1 = rhs[1] - own_high[1] * last
    planes = [
        before,
        block[0] * rest_0 + block[1] * rest_1,
        block[2] * rest_0 + block[3] * rest_1,
        last,
        after,
    ]
    cells = exact_dot(zmat[:, 128 : 128 + wide], jnp.concatenate(planes, 1))
    rims = exact_dot(
        zmat[:, 256 : 256 + CY * wide], jnp.concatenate(planes[1 : CY + 1], 0)
    )
    for k in range(narrow):
        u_send[k, :, 0 : (CY + 2) * LANES] = cells[ZB * k : ZB * (k + 1)]
        u_send[k, :, (CY + 2) * LANES :] = rims[ZB * k : ZB * (k + 1)]
    exchange_narrow(u_send, u_recv, 4)

    locals_[5].wait()
    locals_[6].wait()
    rows = [
        jnp.concatenate(
            [u_recv[k, :, LANES * r : LANES * (r + 1)] for k in range(narrow)], 1
        )
        for r in range(CY + 3)
    ]
    potential = split_dot(jnp.concatenate(rows, 0), ihigh, ilow)
    length_x = potential.shape[1]
    rim = potential[(CY + 2) * ZB :]
    row_id = lax.broadcasted_iota(jnp.int32, (ZB, length_x), 0)

    for y in range(CY):
        here = potential[(y + 1) * ZB : (y + 2) * ZB]
        below = potential[y * ZB : (y + 1) * ZB]
        above = potential[(y + 2) * ZB : (y + 3) * ZB]
        press_ref[y] = here
        left = jnp.where(row_id == 0, rim[2 * y : 2 * y + 1], pltpu.roll(here, 1, 0))
        right = jnp.where(
            row_id == ZB - 1, rim[2 * y + 1 : 2 * y + 2], pltpu.roll(here, ZB - 1, 0)
        )
        grads = [
            pltpu.roll(here, length_x - 1, 1) - pltpu.roll(here, 1, 1),
            above - below,
            right - left,
        ]
        for f in range(3):
            out_ref[f, y] = out_ref[f, y] - 0.5 * grads[f]

    for halo in halos[cut_a:]:
        halo.wait_send()
    part = sums.at[pl.ds(0, 3 * narrow - 1)]
    pltpu.make_async_copy(part, part, phase_send.at[0]).wait()
    for phase, ref in ((1, n_send), (4, u_send)):
        part = ref.at[pl.ds(0, narrow - 1)]
        pltpu.make_async_copy(part, part, phase_send.at[phase]).wait()
    for phase, ref in ((2, w_recv), (3, v_recv)):
        part = ref.at[pl.ds(0, wide - 1)]
        pltpu.make_async_copy(part, part, phase_send.at[phase]).wait()


def body(wide, narrow, consts, fields, y_bands):
    span_here, length_x = fields.shape[2], fields.shape[3]
    tiled = fields.reshape(5, CY, span_here, SUBS, LANES).transpose(0, 1, 3, 2, 4)
    tiled = tiled.reshape(5 * CY * SUBS * span_here, LANES)
    f32 = jnp.float32
    levels = math.ceil(math.log2(wide))
    points = 5 * 5 * (ZB + 2) * SUBS
    vmem = pltpu.VMEM
    scratch = [
        vmem(tiled.shape, f32),
        *[vmem((length_x, length_x), jnp.bfloat16) for _ in range(4)],
        vmem((2 * narrow + 2 * wide, LANES), f32),
        vmem((wide, 512), f32),
        vmem((5, CY + 6, ZB + 6, SUBS, LANES), f32),
        vmem((3, CY + 2, ZB + 4, SUBS, LANES), f32),
        vmem((6, CY, ZB + 2, SUBS, LANES), f32),
        vmem((6, CY, ZB + 2, SUBS, LANES), f32),
        vmem((CY + 2, ZB + 2, SUBS, LANES), f32),
        vmem((3, CY + 2, ZB + 2, SUBS, LANES), f32),
        vmem((points, LANES), f32),
        vmem((points, LANES), f32),
        vmem((points, LANES), f32),
        vmem(((3 * CY + 2) * ZB * SUBS, LANES), f32),
        vmem((3 * narrow, SUBS, LANES), f32),
        vmem((SUBS, LANES), f32),
        vmem((3, wide * CY, LANES), f32),
        vmem((5, wide, LANES), f32),
        vmem((4, wide, LANES), f32),
        vmem((levels, 2, wide, LANES), f32),
        vmem((narrow, ZB, CY * LANES), f32),
        vmem((narrow, ZB, CY * LANES), f32),
        vmem((wide, 2, 1, LANES), f32),
        vmem((wide, 2, 1, LANES), f32),
        vmem((wide, 3, 1, LANES), f32),
        vmem((wide, 3, 1, LANES), f32),
        vmem((narrow, ZB, (CY + 3) * LANES), f32),
        vmem((narrow, ZB, (CY + 3) * LANES), f32),
        pltpu.SemaphoreType.DMA((7,)),
        pltpu.SemaphoreType.REGULAR((wide.bit_length() - 1,)),
        pltpu.SemaphoreType.DMA((24,)),
        pltpu.SemaphoreType.DMA((24,)),
        pltpu.SemaphoreType.DMA((5,)),
        pltpu.SemaphoreType.DMA((5,)),
    ]
    hbm = pl.BlockSpec(memory_space=pltpu.HBM)
    inside = pl.BlockSpec(memory_space=pltpu.VMEM)
    return pl.pallas_call(
        functools.partial(kernel, wide, narrow),
        out_shape=(
            jax.ShapeDtypeStruct(fields.shape, f32),
            jax.ShapeDtypeStruct(fields.shape[1:], f32),
        ),
        in_specs=[hbm, inside, *[hbm] * 5],
        out_specs=(inside, inside),
        scratch_shapes=scratch,
        compiler_params=pltpu.CompilerParams(
            collective_id=0, has_side_effects=True, vmem_limit_bytes=53 * 1024 * 1024
        ),
    )(tiled, y_bands, *consts)


def solution(mesh):
    wide, narrow = mesh.shape["wide"], mesh.shape["narrow"]

    def run(fields, y_bands):
        consts = tables(fields.shape[3], fields.shape[2], wide, narrow)
        consts = [jnp.asarray(table) for table in consts]
        return jax.shard_map(
            functools.partial(body, wide, narrow, consts),
            mesh=mesh,
            in_specs=(P(None, "wide", "narrow", None), P()),
            out_specs=(P(None, "wide", "narrow", None), P("wide", "narrow", None)),
            check_vma=False,
        )(fields, y_bands)

    return run
```
